512 devices in a mesh: pipe: 8 (over x_hi, y), expert: 64 (over z, x_lo, core).
Axes of the slice: x: 4 (x_hi: 2, x_lo: 2; x = x_hi * 2 + x_lo), y: 4, z: 16, core: 2. Of those that a mesh axis runs over, the one named last changes fastest.
Arguments:
- fwd_input: bfloat16 [8, 4096, 3584], P('pipe', 'expert'), may hold values from -6 to 6
- fwd_cotangent: bfloat16 [8, 4096, 3584], P('pipe', 'expert'), may hold values from -6 to 6
- rev_input: bfloat16 [8, 4096, 3584], P('pipe', 'expert'), may hold values from -6 to 6
- rev_cotangent: bfloat16 [8, 4096, 3584], P('pipe', 'expert'), may hold values from -6 to 6
- fwd_routes: int32 [8, 4096, 8], P('pipe', 'expert'), may hold values from 0 to 255, all different within a row; in each aligned block of 64 rows (0 to 63, 64 to 127, ..., all dimensions but the last counted through in order) at most 5 rows name the same one
- rev_routes: int32 [8, 4096, 8], P('pipe', 'expert'), may hold values from 0 to 255, all different within a row; in each aligned block of 64 rows (0 to 63, 64 to 127, ..., all dimensions but the last counted through in order) at most 5 rows name the same one
- fwd_scores: float32 [8, 4096, 8], P('pipe', 'expert'), may hold values from 0.05 to 1
- rev_scores: float32 [8, 4096, 8], P('pipe', 'expert'), may hold values from 0.05 to 1
- norm_gain: float32 [8, 3584], P('pipe'), may hold values from 0.5 to 1.5
- w_gate: bfloat16 [8, 3584, 8192], P('pipe', None, 'expert'), may hold values from -0.09375 to 0.09375
- w_up: bfloat16 [8, 3584, 8192], P('pipe', None, 'expert'), may hold values from -0.09375 to 0.09375
Outputs:
- grad_down: bfloat16 [8, 8192, 3584], P('pipe', 'expert')
The draws below stay inside these ranges and needn't reach their ends.
Inputs may be any that keep to these rules, and one draw needn't show every extreme that they name: `fwd_routes`: in the rows of one device of a micro-batch and group (aligned blocks of 64 rows) no expert is chosen by more than 5 rows; a token's 8 experts differ. `rev_routes`: as fwd_routes.
All inputs are finite; a program needn't handle non-finite values.
Results may differ from the reference program's by a relative error of at most 0.0076.
Values may be sent and summed in bfloat16 or wider, within the bound.
A program may use at most 128 MiB of HBM per device.

```python
import math
from functools import partial
import jax
import jax.numpy as jnp
import numpy as np
from jax import lax

D = 3584
FF = 2048
E_ALL = 256
TOP = 8
TOK_DEV = 64
EXPERTS = 4
TOKENS = 4096
CAP = 5
N_PIPE = 8
N_EXPERT = 64


def level_of(key, dims, cuts, least, largest):
    loudness = 1.0
    for position, blocks in cuts:
        draws = jax.random.uniform(jax.random.fold_in(jax.random.fold_in(key, 6), position), (blocks,), jnp.float32, least / len(cuts), largest / len(cuts))
        loudness = loudness * jnp.repeat(jnp.exp(draws), dims[position] // blocks).reshape((-1,) + (1,) * (len(dims) - 1 - position))
    return loudness


def assign_block(own_key, own, number, rows, amount, top, limit, skew):
    sequence = jax.random.permutation(own_key, amount)
    crowded, ordinary = load_shares(amount, rows * top, limit, skew, True), load_shares(amount, rows * top, limit, skew, False)
    places = jnp.arange(amount)

    def named(tallies, rotation):
        used = int((tallies > 0).sum())
        fixed = max(1, used // 4)
        moved = fixed + (places - fixed + rotation * (used - fixed)) % max(1, amount - fixed)
        return jnp.zeros((amount,), jnp.int32).at[sequence[jnp.where(places < fixed, places, moved)]].set(jnp.asarray(tallies, jnp.int32))

    tallies = jnp.where(number % 4 == 0, named(crowded, number // 4), named(ordinary, number - number // 4 - 1))
    mixed = jax.random.permutation(jax.random.fold_in(own, 3), amount)
    giver, receiver = mixed[0:amount // 2 * 2:2], mixed[1:amount // 2 * 2:2]
    room = jnp.minimum(tallies[giver] - 1, limit - tallies[receiver]) // 2
    room = jnp.where((giver == sequence[0]) | (receiver == sequence[0]) | (tallies[receiver] == 0), 0, jnp.maximum(room, 0))
    moved = jax.random.randint(jax.random.fold_in(own, 4), (amount // 2,), 0, 1 << 20) % (room + 1)
    tallies = tallies.at[giver].add(-moved).at[receiver].add(moved)
    items = jnp.searchsorted(jnp.cumsum(tallies), jnp.arange(rows * top), side="right").astype(jnp.int32)
    grid = items.reshape(top, rows).T
    grid = grid[jax.random.permutation(jax.random.fold_in(own, 1), rows)]
    rotation = jax.random.randint(jax.random.fold_in(own, 2), (rows, 1), 0, top)
    return jnp.take_along_axis(grid, (jnp.arange(top)[None, :] + rotation) % top, axis=1)


def load_shares(count, total, reach, slope, full):
    loads = [(1 << 20) // math.isqrt(standing ** slope) + 1 for standing in range(1, count + 1)]
    largest = reach if full else min(reach, max(-(-total // count), total * loads[0] // sum(loads)))
    least = 1 if total - largest >= count - 1 else 0
    holding, rest = [largest] + [least] * (count - 1), total - largest - least * (count - 1)
    while rest > 0:
        free = [i for i in range(1, count) if holding[i] < largest] or [i for i in range(1, count) if holding[i] < reach]
        pool, budget = sum([loads[i] for i in free]), rest
        for i in free:
            addition = min(reach - holding[i], max(1, budget * loads[i] // pool), rest)
            holding[i] = holding[i] + addition
            rest = rest - addition
    return np.array(holding)


def bell_draw(key, extent, scale, bound, cuts=(), kind=jnp.bfloat16):
    drawn = scale * jax.random.normal(key, extent, jnp.float32)
    if cuts:
        drawn = drawn * level_of(key, extent, cuts, -0.22, 0.18)
    return jnp.clip(drawn, -bound, bound).astype(kind)


def setup_inputs(seed: int = 0) -> dict:
    keys = jax.random.split(jax.random.key(seed), 12)
    fwd_input = bell_draw(keys[0], (N_PIPE, TOKENS, D), 1.0, 6.0, ((0, 8), (1, 64)))
    fwd_cotangent = bell_draw(keys[1], (N_PIPE, TOKENS, D), 1.0, 6.0, ((0, 8), (1, 64)))
    rev_input = bell_draw(keys[2], (N_PIPE, TOKENS, D), 1.0, 6.0, ((0, 8), (1, 64)))
    rev_cotangent = bell_draw(keys[3], (N_PIPE, TOKENS, D), 1.0, 6.0, ((0, 8), (1, 64)))
    fwd_routes_keys = jax.random.split(jax.random.fold_in(keys[4], 1), N_PIPE * TOKENS // TOK_DEV)
    fwd_routes_turns = jax.random.permutation(jax.random.fold_in(keys[4], 3), N_PIPE * TOKENS // TOK_DEV)
    fwd_routes = jax.vmap(lambda own, number: assign_block(jax.random.fold_in(keys[4], 2), own, number, TOK_DEV, E_ALL, TOP, CAP, 1))(fwd_routes_keys, fwd_routes_turns).reshape((N_PIPE, TOKENS, TOP))
    rev_routes_keys = jax.random.split(jax.random.fold_in(keys[5], 1), N_PIPE * TOKENS // TOK_DEV)
    rev_routes_turns = jax.random.permutation(jax.random.fold_in(keys[5], 3), N_PIPE * TOKENS // TOK_DEV)
    rev_routes = jax.vmap(lambda own, number: assign_block(jax.random.fold_in(keys[5], 2), own, number, TOK_DEV, E_ALL, TOP, CAP, 1))(rev_routes_keys, rev_routes_turns).reshape((N_PIPE, TOKENS, TOP))
    fwd_scores = jnp.clip(0.05 + 0.95 * jax.random.uniform(keys[6], (N_PIPE, TOKENS, TOP), jnp.float32) ** level_of(keys[6], (N_PIPE, TOKENS, TOP), ((0, 8), (1, 64)), -0.2, 0.2), 0.05, 1.0)
    rev_scores = jnp.clip(0.05 + 0.95 * jax.random.uniform(keys[7], (N_PIPE, TOKENS, TOP), jnp.float32) ** level_of(keys[7], (N_PIPE, TOKENS, TOP), ((0, 8), (1, 64)), -0.2, 0.2), 0.05, 1.0)
    norm_gain = jnp.clip(1.0 + 0.1 * jax.random.normal(keys[8], (N_PIPE, D), jnp.float32), 0.5, 1.5)
    w_gate = bell_draw(keys[9], (N_PIPE, D, EXPERTS * FF), D ** -0.5, 0.09375, ((0, 8), (2, 64)))
    w_up = bell_draw(keys[10], (N_PIPE, D, EXPERTS * FF), D ** -0.5, 0.09375, ((0, 8), (2, 64)))
    return {"fwd_input": fwd_input, "fwd_cotangent": fwd_cotangent, "rev_input": rev_input, "rev_cotangent": rev_cotangent, "fwd_routes": fwd_routes, "rev_routes": rev_routes, "fwd_scores": fwd_scores, "rev_scores": rev_scores, "norm_gain": norm_gain, "w_gate": w_gate, "w_up": w_up}


def route_weights(routes, scores, experts):
    total = lax.optimization_barrier(jnp.sum(scores, axis=-1, keepdims=True))
    share = 2.5 * scores / total
    hits = (routes[..., None] == jnp.arange(experts, dtype=jnp.int32)).astype(jnp.float32)
    return lax.optimization_barrier(jnp.sum(hits * share[..., None], axis=-2)).astype(jnp.bfloat16)

def pack_rows(tokens, cotangent, weights, gain, capacity):
    values = tokens.astype(jnp.float32)
    normed = (values * lax.rsqrt(lax.optimization_barrier(jnp.mean(values * values, axis=-1, keepdims=True)) + 1e-06) * gain).astype(jnp.bfloat16)
    scaled = (weights.T.astype(jnp.float32)[:, :, None] * cotangent.astype(jnp.float32)[None]).astype(jnp.bfloat16)
    taken = (weights.T > 0).astype(jnp.int32)
    place = jnp.cumsum(taken, axis=1) - 1
    slots = jnp.arange(capacity, dtype=jnp.int32)
    select = ((place[:, None, :] == slots[None, :, None]) & (taken[:, None, :] == 1)).astype(jnp.float32)
    rows = jnp.einsum('ept,td->epd', select, normed.astype(jnp.float32)).astype(jnp.bfloat16)
    grads = jnp.einsum('ept,etd->epd', select, scaled.astype(jnp.float32)).astype(jnp.bfloat16)
    return (rows, grads)

def reference(fwd_input, fwd_cotangent, rev_input, rev_cotangent, fwd_routes, rev_routes, fwd_scores, rev_scores, norm_gain, w_gate, w_up):
    packer = jax.vmap(partial(pack_rows, capacity=CAP), in_axes=(0, 0, 0, None))
    results = []
    for group in range(N_PIPE):
        mirror = N_PIPE - 1 - group
        sources = ((fwd_input[group], fwd_cotangent[group], fwd_routes[group], fwd_scores[group]), (rev_input[mirror], rev_cotangent[mirror], rev_routes[mirror], rev_scores[mirror]))
        row_parts, grad_parts = ([], [])
        for tokens, cotangent, routes, scores in sources:
            weights = route_weights(routes, scores, EXPERTS)
            rows, grads = packer(tokens.reshape(N_EXPERT, TOK_DEV, D), cotangent.reshape(N_EXPERT, TOK_DEV, D), weights.reshape(N_EXPERT, TOK_DEV, EXPERTS), norm_gain[group])
            row_parts.append(rows)
            grad_parts.append(grads)
        rows_all = jnp.concatenate(row_parts, axis=2)
        grads_all = jnp.concatenate(grad_parts, axis=2)
        blocks = []
        for expert in range(EXPERTS):
            flat_rows = rows_all[:, expert].reshape(-1, D)
            flat_grads = grads_all[:, expert].reshape(-1, D)
            gate = jnp.dot(flat_rows, w_gate[group][:, expert * FF:(expert + 1) * FF], preferred_element_type=jnp.float32)
            up = jnp.dot(flat_rows, w_up[group][:, expert * FF:(expert + 1) * FF], preferred_element_type=jnp.float32)
            hidden = (jax.nn.silu(gate) * up).astype(jnp.bfloat16)
            blocks.append(jnp.dot(hidden.T, flat_grads, preferred_element_type=jnp.float32).astype(jnp.bfloat16))
        results.append(jnp.concatenate(blocks, axis=0))
    return jnp.stack(results)
```

```python
import functools

import jax
import jax.numpy as jnp
from jax import lax
from jax.experimental import pallas as pl
from jax.experimental.pallas import tpu as pltpu
from jax.sharding import PartitionSpec as P

MESH = pl.DeviceIdType.MESH
D = 3584
TOK = 64
CAP = 5
PARTS = 4
LANES = D // PARTS
ROWS = 80
HID = 128


def iota(shape, axis):
    return lax.broadcasted_iota(jnp.int32, shape, axis)


def select_tables(routes, scores, core):
    share = 2.5 * scores / jnp.sum(scores, axis=0, keepdims=True)
    row = iota((8, TOK), 0)
    coef = jnp.zeros((8, TOK), jnp.float32)
    for e in range(4):
        mine = jnp.sum(jnp.where(routes == e, share, 0.0), axis=0, keepdims=True)
        coef = coef + jnp.where(row == e, mine, 0.0)
    coef = coef.astype(jnp.bfloat16)
    taken = jnp.where(coef.astype(jnp.float32) > 0, 1.0, 0.0).astype(jnp.bfloat16)
    token, lane = iota((TOK, 128), 0), iota((TOK, 128), 1) % TOK
    upto = jnp.where(token <= lane, 1.0, 0.0).astype(jnp.bfloat16)
    same = jnp.where(token == lane, 1.0, 0.0).astype(jnp.bfloat16)
    place = jnp.dot(taken, upto, preferred_element_type=jnp.float32) - 1.0
    weight = jnp.dot(coef, same, preferred_element_type=jnp.float32)
    r, lane = iota((16, 128), 0), iota((16, 128), 1)
    left = lane < TOK
    first = CAP * core
    main_ok = left == (r % 16 < 8)
    main_slot = (r % 8 - first).astype(jnp.float32)
    rem_ok = left == (r % 4 < 2)
    rem_slot = (8 + r % 2 - first).astype(jnp.float32)
    main, rem = [], []
    for e in range(4):
        where = jnp.broadcast_to(place[e : e + 1], (16, 128))
        much = jnp.broadcast_to(weight[e : e + 1], (16, 128))
        value = jnp.where(much > 0, jnp.where(left, 1.0, much), 0.0)
        main.append(jnp.where(main_ok & (where == main_slot), value, 0.0))
        rem.append(jnp.where(rem_ok & (where == rem_slot), value, 0.0))
    return jnp.concatenate(main, axis=0), jnp.concatenate(rem, axis=0)


def pack(mb, routes_ref, scores_ref, gain, core, raw, data, packed):
    main, rem = select_tables(routes_ref[...], scores_ref[...], core)
    values = raw[mb].astype(jnp.float32)
    scale = lax.rsqrt(jnp.mean(values * values, axis=-1, keepdims=True) + 1e-06)
    data[mb, 0:TOK, :] = (values * scale * gain).astype(jnp.bfloat16)
    part = (iota((64, 128), 0) % 16) // 4
    total = jnp.zeros((64, LANES), jnp.float32)
    for p in range(PARTS):
        lhs = jnp.concatenate([main, jnp.where(part == p, rem, 0.0)], axis=0).astype(jnp.bfloat16)
        rows = jnp.dot(
            lhs, data[mb, :, p * LANES : (p + 1) * LANES], preferred_element_type=jnp.float32
        )
        packed[mb, :, 16 * p : 16 * p + 16, :] = (
            rows[:64].astype(jnp.bfloat16).reshape(4, 16, LANES)
        )
        total = total + rows[64:]
    packed[mb, :, 64:80, :] = total.astype(jnp.bfloat16).reshape(4, 16, LANES)


def kernel(
    fx, fg, rx, rg, f_routes, r_routes, f_scores, r_scores, gain_ref, wg, wu, out_ref,
    buf, raw, data, packed, gathered, weights, spare, grad, gain_in,
    load_sem, local_sem, gain_sem, swap_sem, first_sem, right_sem, left_sem, x_sem, core_sem, recv_sem,
):
    pipe = lax.axis_index("pipe")
    me = lax.axis_index("expert")
    z, x_lo, core = me // 4, (me // 2) % 2, me % 2
    q, i = z // 4, z % 4
    col = x_lo * 2 + core
    xcol = (1 - x_lo) * 2 + core
    half = i // 2

    def at(zz, xx, cc, pp=None):
        return (pipe if pp is None else pp, zz * 4 + xx * 2 + cc)

    far_pipe = pipe * (1 - core) + (7 - pipe) * core
    far_x = x_lo * (1 - core) + (1 - x_lo) * core
    mirror = at(z, 1 - x_lo, core, 7 - pipe)
    core_mate = at(z, x_lo, 1 - core)
    x_mate = at(z, 1 - x_lo, core)
    z_right = at((z + 1) % 16, x_lo, core)
    z_left = at((z + 15) % 16, x_lo, core)

    loads = [
        pltpu.make_async_copy(fx.at[0], raw.at[0], load_sem.at[0]),
        pltpu.make_async_copy(fg.at[0], data.at[0, pl.ds(TOK, TOK)], load_sem.at[1]),
        pltpu.make_async_copy(rx.at[0], raw.at[1], load_sem.at[2]),
        pltpu.make_async_copy(rg.at[0], data.at[1, pl.ds(TOK, TOK)], load_sem.at[3]),
        pltpu.make_async_copy(wg.at[0], weights.at[:, pl.ds(0, HID)], load_sem.at[4]),
        pltpu.make_async_copy(wu.at[0], weights.at[:, pl.ds(HID, HID)], load_sem.at[5]),
    ]
    for load in loads:
        load.start()

    barrier = pltpu.get_barrier_semaphore()

    def greet(device):
        pl.semaphore_signal(barrier, inc=1, device_id=device, device_id_type=MESH)

    greet(core_mate)
    greet(x_mate)
    greet(mirror)

    @pl.when(i > 0)
    def _():
        greet(z_left)

    @pl.when(i < 3)
    def _():
        greet(z_right)

    @pl.when(i == 0)
    def _():
        for k in range(4):
            greet(at(((q + 3) % 4) * 4 + k, far_x, core, far_pipe))
        for k in (2, 3):
            greet(at(((q + 2) % 4) * 4 + k, far_x, core, far_pipe))

    @pl.when(i == 3)
    def _():
        for k in range(4):
            greet(at(((q + 1) % 4) * 4 + k, far_x, core, far_pipe))
        for k in (0, 1):
            greet(at(((q + 2) % 4) * 4 + k, far_x, core, far_pipe))

    loads[0].wait()
    loads[1].wait()
    pack(0, f_routes, f_scores, gain_ref[...], core, raw, data, packed)
    pl.semaphore_wait(barrier, 7 + (i * (3 - i)) // 2)

    def remote(src, dst, send, recv, device):
        return pltpu.make_async_remote_copy(
            src_ref=src, dst_ref=dst, send_sem=send, recv_sem=recv, device_id=device, device_id_type=MESH
        )

    gain_copy = remote(gain_ref, gain_in, gain_sem.at[0], gain_sem.at[1], mirror)
    gain_copy.start()
    swap = remote(packed.at[1 - core], gathered, swap_sem.at[0], swap_sem.at[1], core_mate)

    def forward(slot, c, send, device):
        return remote(buf.at[slot, c], buf.at[slot, c], send, recv_sem.at[slot, c], device)

    def arrived(slot, c):
        forward(slot, c, core_sem.at[slot, 0], core_mate).wait_recv()

    def go_right(slot):
        return forward(slot, col, right_sem.at[slot], z_right)

    def go_left(slot):
        return forward(slot, col, left_sem.at[slot], z_left)

    def go_x(slot):
        return forward(slot, col, x_sem.at[slot], x_mate)

    def go_core(slot, c, which):
        return forward(slot, c, core_sem.at[slot, which], core_mate)

    far_col = far_x * 2 + core

    def first(step, zz, slot):
        return remote(
            packed.at[core, (q + step) % 4], buf.at[slot, far_col], first_sem.at[step],
            recv_sem.at[slot, far_col], at(zz, far_x, core, far_pipe),
        )

    to_right = first(1, ((q + 1) % 4) * 4, 7 - i + 2 * (1 - half))
    to_left = first(3, ((q + 3) % 4) * 4 + 3, 6 + i + 2 * half)
    to_across = first(
        2, ((q + 2) % 4) * 4 + 3 * (1 - half), half * (15 - i) + (1 - half) * (14 + i)
    )
    to_mirror = first(0, z, i)
    keep = pltpu.make_async_copy(packed.at[0, q], buf.at[i, col], local_sem)

    def merge():
        packed[core] = packed[core] + gathered[...]

    def spread_own():
        @pl.when(i < 3)
        def _():
            go_right(i).start()

        @pl.when(i > 0)
        def _():
            go_left(i).start()

        go_x(i).start()
        go_core(i, col, 0).start()

    @pl.when(core == 1)
    def _():
        swap.start()

    @pl.when(core == 0)
    def _():
        swap.wait_recv()
        merge()
        keep.start()
        to_right.start()
        to_left.start()
        to_across.start()
        keep.wait()
        spread_own()

    loads[2].wait()
    loads[3].wait()
    gain_copy.wait_recv()
    pack(1, r_routes, r_scores, gain_in[...], core, raw, data, packed)

    @pl.when(core == 0)
    def _():
        swap.start()

    @pl.when(core == 1)
    def _():
        swap.wait_recv()
        merge()
        to_mirror.start()
        to_right.start()
        to_left.start()
        to_across.start()

    grad[...] = jnp.zeros_like(grad)

    @pl.when(core == 1)
    def _():
        arrived(i, col)
        spread_own()

    def from_left(slot):
        arrived(slot, col)

        @pl.when(i < 3)
        def _():
            go_right(slot).start()

        go_x(slot).start()
        go_core(slot, col, 0).start()

    def from_right(slot):
        arrived(slot, col)

        @pl.when(i > 0)
        def _():
            go_left(slot).start()

        go_x(slot).start()
        go_core(slot, col, 0).start()

    for step in range(1, 4):

        @pl.when(i >= step)
        def _():
            from_left(i - step)

        @pl.when(i + step <= 3)
        def _():
            from_right(i + step)

    def from_x(slot):
        arrived(slot, xcol)
        go_core(slot, xcol, 1).start()

    def compute(phase):
        block = pl.ds(4 * phase, 4)
        for slot in range(4 * phase, 4 * phase + 4):
            arrived(slot, x_lo * 2 + 1 - core)
            arrived(slot, (1 - x_lo) * 2 + 1 - core)
        out_row, in_row = iota((256, 256), 0), iota((256, 256), 1)
        source = ((out_row % 64) // 4) * 16 + (out_row // 64) * 4 + out_row % 4
        turn = jnp.where(in_row == source, 1.0, 0.0).astype(jnp.bfloat16)
        tail = buf[block, :, 64:80, :].reshape(256, LANES)
        spare[...] = jnp.dot(turn, tail, preferred_element_type=jnp.float32).astype(jnp.bfloat16)
        both = jnp.zeros((320, 2 * HID), jnp.float32)
        for p in range(PARTS):
            rows = jnp.concatenate(
                [
                    buf[block, :, 16 * p : 16 * p + 16, :].reshape(256, LANES),
                    spare[64 * p : 64 * p + 64, :],
                ],
                axis=0,
            )
            both = both + jnp.dot(
                rows, weights[p * LANES : (p + 1) * LANES, :], preferred_element_type=jnp.float32
            )
        gate, up = both[:, :HID], both[:, HID:]
        hidden = gate / (1.0 + jnp.exp(-gate)) * up
        row = iota((320, HID), 0)
        moved = jnp.concatenate(
            [pltpu.roll(hidden[:256], 8, 0), pltpu.roll(hidden[256:], 2, 0)], axis=0
        )
        valid = ((row < 256) & (row % 16 >= 8)) | ((row >= 256) & (row % 4 >= 2))
        side = jnp.where(valid, moved, 0.0).T.astype(jnp.bfloat16)
        for p in range(PARTS):
            rows = jnp.concatenate(
                [
                    buf[block, :, 16 * p : 16 * p + 16, :].reshape(256, LANES),
                    spare[64 * p : 64 * p + 64, :],
                ],
                axis=0,
            )
            lanes = slice(p * LANES, (p + 1) * LANES)
            grad[:, lanes] += jnp.dot(side, rows, preferred_element_type=jnp.float32)

    loads[4].wait()
    loads[5].wait()
    for phase in range(1, 4):
        for k, slot in enumerate((4 * phase, 4 * phase + 2, 4 * phase + 1, 4 * phase + 3)):
            (from_left if k % 2 == 0 else from_right)(slot)
            from_x(4 * phase - 4 + k)
        compute(phase - 1)
    for slot in (12, 14, 13, 15):
        from_x(slot)
    compute(3)
    out_ref[0] = grad[...].astype(jnp.bfloat16)

    gain_copy.wait_send()
    swap.wait_send()
    to_right.wait_send()
    to_left.wait_send()
    to_across.wait_send()

    @pl.when(core == 1)
    def _():
        to_mirror.wait_send()

    for slot in range(16):
        go_x(slot).wait_send()
        go_core(slot, col, 0).wait_send()
        go_core(slot, xcol, 1).wait_send()
    for slot in range(4):

        @pl.when((slot <= i) & (i < 3))
        def _():
            go_right(slot).wait_send()

        @pl.when((slot >= i) & (i > 0))
        def _():
            go_left(slot).wait_send()

    @pl.when(i < 3)
    def _():
        for slot in (4, 5, 8, 9, 12, 13):
            go_right(slot).wait_send()

    @pl.when(i > 0)
    def _():
        for slot in (6, 7, 10, 11, 14, 15):
            go_left(slot).wait_send()


def body(fx, fg, rx, rg, f_routes, r_routes, f_scores, r_scores, gain, w_gate, w_up):
    vmem, hbm = pl.BlockSpec(memory_space=pltpu.VMEM), pl.BlockSpec(memory_space=pl.ANY)
    dma = pltpu.SemaphoreType.DMA
    return pl.pallas_call(
        kernel,
        name="routed_grad",
        out_shape=jax.ShapeDtypeStruct((1, HID, D), jnp.bfloat16),
        in_specs=[hbm] * 4 + [vmem] * 5 + [hbm] * 2,
        out_specs=vmem,
        scratch_shapes=[
            pltpu.VMEM((16, 4, ROWS, LANES), jnp.bfloat16),
            pltpu.VMEM((2, TOK, D), jnp.bfloat16),
            pltpu.VMEM((2, 2 * TOK, D), jnp.bfloat16),
            pltpu.VMEM((2, 4, ROWS, LANES), jnp.bfloat16),
            pltpu.VMEM((4, ROWS, LANES), jnp.bfloat16),
            pltpu.VMEM((D, 2 * HID), jnp.bfloat16),
            pltpu.VMEM((256, LANES), jnp.bfloat16),
            pltpu.VMEM((HID, D), jnp.float32),
            pltpu.VMEM((1, D), jnp.float32),
            dma((6,)), dma, dma((2,)), dma((2,)), dma((4,)), dma((16,)), dma((16,)), dma((16,)),
            dma((16, 2)), dma((16, 4)),
        ],
        compiler_params=pltpu.CompilerParams(
            collective_id=0, has_side_effects=True, vmem_limit_bytes=48 << 20
        ),
        cost_estimate=pl.CostEstimate(flops=6 << 30, bytes_accessed=5 << 20, transcendentals=1 << 17),
    )(
        fx, fg, rx, rg, f_routes[0].T, r_routes[0].T, f_scores[0].T, r_scores[0].T, gain, w_gate, w_up
    )


def solution(mesh):
    rows = P("pipe", "expert", None)
    in_specs = (rows,) * 8 + (P("pipe", None),) + (P("pipe", None, "expert"),) * 2
    return jax.shard_map(body, mesh=mesh, in_specs=in_specs, out_specs=rows, check_vma=False)
```

```python
import functools

import jax
import jax.numpy as jnp
from jax import lax
from jax.experimental import pallas as pl
from jax.experimental.pallas import tpu as pltpu
from jax.sharding import PartitionSpec as P

MESH = pl.DeviceIdType.MESH
D = 3584
TOK = 64
CAP = 5
PARTS = 4
LANES = D // PARTS
ROWS = 80
HID = 128


def iota(shape, axis):
    return lax.broadcasted_iota(jnp.int32, shape, axis)


def select_tables(routes, scores, core):
    share = 2.5 * scores / jnp.sum(scores, axis=0, keepdims=True)
    row = iota((8, TOK), 0)
    coef = jnp.zeros((8, TOK), jnp.float32)
    for e in range(4):
        mine = jnp.sum(jnp.where(routes == e, share, 0.0), axis=0, keepdims=True)
        coef = coef + jnp.where(row == e, mine, 0.0)
    coef = coef.astype(jnp.bfloat16)
    taken = jnp.where(coef.astype(jnp.float32) > 0, 1.0, 0.0).astype(jnp.bfloat16)
    token, lane = iota((TOK, 128), 0), iota((TOK, 128), 1) % TOK
    upto = jnp.where(token <= lane, 1.0, 0.0).astype(jnp.bfloat16)
    same = jnp.where(token == lane, 1.0, 0.0).astype(jnp.bfloat16)
    place = jnp.dot(taken, upto, preferred_element_type=jnp.float32) - 1.0
    weight = jnp.dot(coef, same, preferred_element_type=jnp.float32)
    r, lane = iota((16, 128), 0), iota((16, 128), 1)
    left = lane < TOK
    first = CAP * core
    main_ok = left == (r % 16 < 8)
    main_slot = (r % 8 - first).astype(jnp.float32)
    rem_ok = left == (r % 4 < 2)
    rem_slot = (8 + r % 2 - first).astype(jnp.float32)
    main, rem = [], []
    for e in range(4):
        where = jnp.broadcast_to(place[e : e + 1], (16, 128))
        much = jnp.broadcast_to(weight[e : e + 1], (16, 128))
        value = jnp.where(much > 0, jnp.where(left, 1.0, much), 0.0)
        main.append(jnp.where(main_ok & (where == main_slot), value, 0.0))
        rem.append(jnp.where(rem_ok & (where == rem_slot), value, 0.0))
    return jnp.concatenate(main, axis=0), jnp.concatenate(rem, axis=0)


def pack(mb, routes, scores, gain, core, raw, data, packed):
    main, rem = select_tables(routes, scores, core)
    values = raw[mb].astype(jnp.float32)
    scale = lax.rsqrt(jnp.mean(values * values, axis=-1, keepdims=True) + 1e-06)
    data[mb, 0:TOK, :] = (values * scale * gain).astype(jnp.bfloat16)
    part = (iota((64, 128), 0) % 16) // 4
    total = jnp.zeros((64, LANES), jnp.float32)
    for p in range(PARTS):
        lhs = jnp.concatenate([main, jnp.where(part == p, rem, 0.0)], axis=0).astype(jnp.bfloat16)
        rows = jnp.dot(
            lhs, data[mb, :, p * LANES : (p + 1) * LANES], preferred_element_type=jnp.float32
        )
        packed[mb, :, 16 * p : 16 * p + 16, :] = (
            rows[:64].astype(jnp.bfloat16).reshape(4, 16, LANES)
        )
        total = total + rows[64:]
    packed[mb, :, 64:80, :] = total.astype(jnp.bfloat16).reshape(4, 16, LANES)


def kernel(
    fx, fg, rx, rg, routes_0, routes_1, scores_0, scores_1, gain_0, wg, wu, out_ref,
    buf, routes, scores, gain_ref, raw, data, packed, gathered, weights, spare, grad, gain_in,
    load_sem, local_sem, gain_sem, swap_sem, first_sem, right_sem, left_sem, x_sem, core_sem, recv_sem,
):
    pipe = lax.axis_index("pipe")
    me = lax.axis_index("expert")
    z, x_lo, core = me // 4, (me // 2) % 2, me % 2
    q, i = z // 4, z % 4
    col = x_lo * 2 + core
    xcol = (1 - x_lo) * 2 + core
    half = i // 2

    def at(zz, xx, cc, pp=None):
        return (pipe if pp is None else pp, zz * 4 + xx * 2 + cc)

    far_pipe = pipe * (1 - core) + (lax.axis_size("pipe") - 1 - pipe) * core
    far_x = x_lo * (1 - core) + (1 - x_lo) * core
    mirror = at(z, 1 - x_lo, core, lax.axis_size("pipe") - 1 - pipe)
    core_mate = at(z, x_lo, 1 - core)
    x_mate = at(z, 1 - x_lo, core)
    z_right = at((z + 1) % 16, x_lo, core)
    z_left = at((z + 15) % 16, x_lo, core)

    sources = (
        (routes_0, routes.at[0]),
        (scores_0, scores.at[0]),
        (fx.at[0], raw.at[0]),
        (gain_0, gain_ref),
        (fg.at[0], data.at[0, pl.ds(TOK, TOK)]),
        (routes_1, routes.at[1]),
        (scores_1, scores.at[1]),
        (rx.at[0], raw.at[1]),
        (rg.at[0], data.at[1, pl.ds(TOK, TOK)]),
        (wg.at[0], weights.at[:, pl.ds(0, HID)]),
        (wu.at[0], weights.at[:, pl.ds(HID, HID)]),
    )
    loads = [pltpu.make_async_copy(a, b, load_sem.at[k]) for k, (a, b) in enumerate(sources)]
    for load in loads:
        load.start()

    barrier = pltpu.get_barrier_semaphore()

    def greet(device):
        pl.semaphore_signal(barrier, inc=1, device_id=device, device_id_type=MESH)

    greet(core_mate)
    greet(x_mate)
    greet(mirror)

    @pl.when(i > 0)
    def _():
        greet(z_left)

    @pl.when(i < 3)
    def _():
        greet(z_right)

    @pl.when(i == 0)
    def _():
        for k in range(4):
            greet(at(((q + 3) % 4) * 4 + k, far_x, core, far_pipe))
        for k in (2, 3):
            greet(at(((q + 2) % 4) * 4 + k, far_x, core, far_pipe))

    @pl.when(i == 3)
    def _():
        for k in range(4):
            greet(at(((q + 1) % 4) * 4 + k, far_x, core, far_pipe))
        for k in (0, 1):
            greet(at(((q + 2) % 4) * 4 + k, far_x, core, far_pipe))

    for load in loads[:5]:
        load.wait()
    pack(0, routes[0], scores[0], gain_ref[...], core, raw, data, packed)
    pl.semaphore_wait(barrier, 7 + (i * (3 - i)) // 2)

    def remote(src, dst, send, recv, device):
        return pltpu.make_async_remote_copy(
            src_ref=src, dst_ref=dst, send_sem=send, recv_sem=recv, device_id=device, device_id_type=MESH
        )

    gain_copy = remote(gain_ref, gain_in, gain_sem.at[0], gain_sem.at[1], mirror)
    gain_copy.start()
    swap = remote(packed.at[1 - core], gathered, swap_sem.at[0], swap_sem.at[1], core_mate)

    def forward(slot, c, send, device):
        return remote(buf.at[slot, c], buf.at[slot, c], send, recv_sem.at[slot, c], device)

    def arrived(slot, c):
        forward(slot, c, core_sem.at[slot, 0], core_mate).wait_recv()

    def go_right(slot):
        return forward(slot, col, right_sem.at[slot], z_right)

    def go_left(slot):
        return forward(slot, col, left_sem.at[slot], z_left)

    def go_x(slot):
        return forward(slot, col, x_sem.at[slot], x_mate)

    def go_core(slot, c, which):
        return forward(slot, c, core_sem.at[slot, which], core_mate)

    far_col = far_x * 2 + core

    def first(step, zz, slot):
        return remote(
            packed.at[core, (q + step) % 4], buf.at[slot, far_col], first_sem.at[step],
            recv_sem.at[slot, far_col], at(zz, far_x, core, far_pipe),
        )

    own = 9 - i
    to_right = first(1, ((q + 1) % 4) * 4, 13 - i)
    to_left = first(3, ((q + 3) % 4) * 4 + 3, 5 - i)
    to_across = first(
        2, ((q + 2) % 4) * 4 + 3 * (1 - half), half * (17 - i) + (1 - half) * (1 - i)
    )
    to_mirror = first(0, z, own)
    keep = pltpu.make_async_copy(packed.at[0, q], buf.at[own, col], local_sem)

    def merge():
        packed[core] = packed[core] + gathered[...]

    def spread_own():
        @pl.when(i < 3)
        def _():
            go_right(own).start()

        @pl.when(i > 0)
        def _():
            go_left(own).start()

        go_x(own).start()
        go_core(own, col, 0).start()

    @pl.when(core == 1)
    def _():
        swap.start()

    @pl.when(core == 0)
    def _():
        swap.wait_recv()
        merge()
        keep.start()
        to_right.start()
        to_left.start()
        keep.wait()
        spread_own()
        to_across.start()

    for load in loads[5:9]:
        load.wait()
    gain_copy.wait_recv()
    pack(1, routes[1], scores[1], gain_in[...], core, raw, data, packed)

    @pl.when(core == 0)
    def _():
        swap.start()

    @pl.when(core == 1)
    def _():
        swap.wait_recv()
        merge()
        to_mirror.start()
        to_right.start()
        to_left.start()
        to_across.start()

    grad[...] = jnp.zeros_like(grad)

    @pl.when(core == 1)
    def _():
        arrived(own, col)
        spread_own()

    def from_left(slot):
        arrived(slot, col)

        @pl.when(i < 3)
        def _():
            go_right(slot).start()

        go_x(slot).start()
        go_core(slot, col, 0).start()

    def from_right(slot):
        arrived(slot, col)

        @pl.when(i > 0)
        def _():
            go_left(slot).start()

        go_x(slot).start()
        go_core(slot, col, 0).start()

    def from_x(slot):
        arrived(slot, xcol)
        go_core(slot, xcol, 1).start()

    def compute(phase):
        block = pl.ds(4 * phase, 4)
        for k in range(4):
            arrived(4 * phase + k, x_lo * 2 + 1 - core)
            arrived(4 * phase + k, (1 - x_lo) * 2 + 1 - core)
        out_row, in_row = iota((256, 256), 0), iota((256, 256), 1)
        source = ((out_row % 64) // 4) * 16 + (out_row // 64) * 4 + out_row % 4
        turn = jnp.where(in_row == source, 1.0, 0.0).astype(jnp.bfloat16)
        tail = buf[block, :, 64:80, :].reshape(256, LANES)
        spare[...] = jnp.dot(turn, tail, preferred_element_type=jnp.float32).astype(jnp.bfloat16)
        both = jnp.zeros((320, 2 * HID), jnp.float32)
        for p in range(PARTS):
            rows = jnp.concatenate(
                [
                    buf[block, :, 16 * p : 16 * p + 16, :].reshape(256, LANES),
                    spare[64 * p : 64 * p + 64, :],
                ],
                axis=0,
            )
            both = both + jnp.dot(
                rows, weights[p * LANES : (p + 1) * LANES, :], preferred_element_type=jnp.float32
            )
        gate, up = both[:, :HID], both[:, HID:]
        hidden = gate / (1.0 + jnp.exp(-gate)) * up
        row = iota((320, HID), 0)
        moved = jnp.concatenate(
            [pltpu.roll(hidden[:256], 8, 0), pltpu.roll(hidden[256:], 2, 0)], axis=0
        )
        valid = ((row < 256) & (row % 16 >= 8)) | ((row >= 256) & (row % 4 >= 2))
        side = jnp.where(valid, moved, 0.0).T.astype(jnp.bfloat16)
        for p in range(PARTS):
            rows = jnp.concatenate(
                [
                    buf[block, :, 16 * p : 16 * p + 16, :].reshape(256, LANES),
                    spare[64 * p : 64 * p + 64, :],
                ],
                axis=0,
            )
            lanes = slice(p * LANES, (p + 1) * LANES)
            grad[:, lanes] += jnp.dot(side, rows, preferred_element_type=jnp.float32)

    for load in loads[9:]:
        load.wait()
    def along_x(step):
        if step < 0:
            from_x(own)
            return

        @pl.when(step <= 5 + i)
        def _():
            from_x(own + 1 + step)

        @pl.when(step <= 8 - i)
        def _():
            from_x(own - 1 - step)

    for step in range(9):

        @pl.when(step <= 5 + i)
        def _():
            from_left(own + 1 + step)

        @pl.when(step <= 8 - i)
        def _():
            from_right(own - 1 - step)

        along_x(step - 1)
        if step == 4:
            compute(2 - half)
        if step == 6:
            compute(1 + half)
        if step == 8:
            compute(3 - 3 * half)
    along_x(8)
    compute(3 * half)
    out_ref[0] = grad[...].astype(jnp.bfloat16)

    gain_copy.wait_send()
    swap.wait_send()
    to_right.wait_send()
    to_left.wait_send()
    to_across.wait_send()

    @pl.when(core == 1)
    def _():
        to_mirror.wait_send()

    for slot in range(16):
        go_x(slot).wait_send()
        go_core(slot, col, 0).wait_send()
        go_core(slot, xcol, 1).wait_send()
    for slot in range(16):

        @pl.when((slot >= own) & (i < 3))
        def _():
            go_right(slot).wait_send()

        @pl.when((slot <= own) & (i > 0))
        def _():
            go_left(slot).wait_send()


def body(fx, fg, rx, rg, f_routes, r_routes, f_scores, r_scores, gain, w_gate, w_up):
    vmem, hbm = pl.BlockSpec(memory_space=pltpu.VMEM), pl.BlockSpec(memory_space=pl.ANY)
    dma = pltpu.SemaphoreType.DMA
    return pl.pallas_call(
        kernel,
        name="routed_grad",
        out_shape=jax.ShapeDtypeStruct((1, HID, D), jnp.bfloat16),
        in_specs=[hbm] * 11,
        out_specs=vmem,
        scratch_shapes=[
            pltpu.VMEM((16, 4, ROWS, LANES), jnp.bfloat16),
            pltpu.VMEM((2, 8, TOK), jnp.int32),
            pltpu.VMEM((2, 8, TOK), jnp.float32),
            pltpu.VMEM((1, D), jnp.float32),
            pltpu.VMEM((2, TOK, D), jnp.bfloat16),
            pltpu.VMEM((2, 2 * TOK, D), jnp.bfloat16),
            pltpu.VMEM((2, 4, ROWS, LANES), jnp.bfloat16),
            pltpu.VMEM((4, ROWS, LANES), jnp.bfloat16),
            pltpu.VMEM((D, 2 * HID), jnp.bfloat16),
            pltpu.VMEM((256, LANES), jnp.bfloat16),
            pltpu.VMEM((HID, D), jnp.float32),
            pltpu.VMEM((1, D), jnp.float32),
            dma((11,)), dma, dma((2,)), dma((2,)), dma((4,)), dma((16,)), dma((16,)), dma((16,)),
            dma((16, 2)), dma((16, 4)),
        ],
        compiler_params=pltpu.CompilerParams(
            collective_id=0, has_side_effects=True, vmem_limit_bytes=63 << 20
        ),
        cost_estimate=pl.CostEstimate(flops=6 << 30, bytes_accessed=5 << 20, transcendentals=1 << 17),
    )(
        fx, fg, rx, rg, f_routes[0].T, r_routes[0].T, f_scores[0].T, r_scores[0].T, gain, w_gate, w_up
    )


def solution(mesh):
    rows = P("pipe", "expert", None)
    in_specs = (rows,) * 8 + (P("pipe", None),) + (P("pipe", None, "expert"),) * 2
    return jax.shard_map(body, mesh=mesh, in_specs=in_specs, out_specs=rows, check_vma=False)
```

```python
import functools

import jax
import jax.numpy as jnp
from jax import lax
from jax.experimental import pallas as pl
from jax.experimental.pallas import tpu as pltpu
from jax.sharding import PartitionSpec as P

MESH = pl.DeviceIdType.MESH
AHEAD = 1
D = 3584
TOK = 64
CAP = 5
PARTS = 4
LANES = D // PARTS
ROWS = 80
HID = 128


def iota(shape, axis):
    return lax.broadcasted_iota(jnp.int32, shape, axis)


def select_tables(routes_ref, scores_ref):
    place = jnp.zeros((8, 4 * TOK), jnp.float32)
    weight = jnp.zeros((8, 4 * TOK), jnp.float32)
    row = iota((8, TOK), 0)
    token, lane = iota((TOK, 4 * TOK), 0), iota((TOK, 4 * TOK), 1)
    for h in range(2):
        routes, scores = routes_ref[h], scores_ref[h]
        share = 2.5 * scores / jnp.sum(scores, axis=0, keepdims=True)
        coef = jnp.zeros((8, TOK), jnp.float32)
        for e in range(4):
            mine = jnp.sum(jnp.where(routes == e, share, 0.0), axis=0, keepdims=True)
            coef = coef + jnp.where(row == e, mine, 0.0)
        coef = coef.astype(jnp.bfloat16)
        taken = jnp.where(coef.astype(jnp.float32) > 0, 1.0, 0.0).astype(jnp.bfloat16)
        here = (lane // TOK) % 2 == h
        upto = jnp.where(here & (token <= lane % TOK), 1.0, 0.0).astype(jnp.bfloat16)
        same = jnp.where(here & (token == lane % TOK), 1.0, 0.0).astype(jnp.bfloat16)
        place = place + jnp.dot(taken, upto, preferred_element_type=jnp.float32)
        weight = weight + jnp.dot(coef, same, preferred_element_type=jnp.float32)
    lane = iota((8, 4 * TOK), 1)
    place = place + jnp.where((lane // TOK) % 2 == 1, CAP - 1.0, -1.0)
    r, lane = iota((16, 4 * TOK), 0), iota((16, 4 * TOK), 1)
    left = lane < 2 * TOK
    main_ok = left == (r < 8)
    main_slot = (r % 8).astype(jnp.float32)
    rem_ok = left == (r % 4 < 2)
    rem_slot = (8 + r % 2).astype(jnp.float32)
    main, rem = [], []
    for e in range(4):
        where = jnp.broadcast_to(place[e : e + 1], (16, 4 * TOK))
        much = jnp.broadcast_to(weight[e : e + 1], (16, 4 * TOK))
        value = jnp.where(much > 0, jnp.where(left, 1.0, much), 0.0)
        main.append(jnp.where(main_ok & (where == main_slot), value, 0.0))
        rem.append(jnp.where(rem_ok & (where == rem_slot), value, 0.0))
    return jnp.concatenate(main, axis=0), jnp.concatenate(rem, axis=0)


def pack(main, rem, data, packed):
    part = (iota((64, 4 * TOK), 0) % 16) // 4
    total = jnp.zeros((64, LANES), jnp.float32)
    for p in range(PARTS):
        lhs = jnp.concatenate([main, jnp.where(part == p, rem, 0.0)], axis=0).astype(jnp.bfloat16)
        rows = jnp.dot(
            lhs, data[:, p * LANES : (p + 1) * LANES], preferred_element_type=jnp.float32
        )
        packed[:, 16 * p : 16 * p + 16, :] = rows[:64].astype(jnp.bfloat16).reshape(4, 16, LANES)
        total = total + rows[64:]
    packed[:, 64:80, :] = total.astype(jnp.bfloat16).reshape(4, 16, LANES)


def kernel(
    fx, fg, rx, rg, routes_0, routes_1, scores_0, scores_1, gain_0, wg, wu, out_ref,
    buf, routes, scores, gain, gain_in, raw, data, packed, weights, spare, grad,
    load_sem, local_sem, gain_sem, swap_send, swap_recv, first_sem, right_sem, left_sem, x_sem, core_sem, recv_sem,
):
    pipe = lax.axis_index("pipe")
    me = lax.axis_index("expert")
    z, x_lo, core = me // 4, (me // 2) % 2, me % 2
    q, i = z // 4, z % 4
    col = x_lo * 2 + core
    xcol = (1 - x_lo) * 2 + core
    half = i // 2

    def at(zz, xx, cc, pp=None):
        return (pipe if pp is None else pp, zz * 4 + xx * 2 + cc)

    far_pipe = pipe * (1 - core) + (lax.axis_size("pipe") - 1 - pipe) * core
    far_x = x_lo * (1 - core) + (1 - x_lo) * core
    mirror = at(z, 1 - x_lo, core, lax.axis_size("pipe") - 1 - pipe)
    core_mate = at(z, x_lo, 1 - core)
    x_mate = at(z, 1 - x_lo, core)
    z_right = at((z + 1) % 16, x_lo, core)
    z_left = at((z + 15) % 16, x_lo, core)

    def load(k, source, target):
        return pltpu.make_async_copy(source, target, load_sem.at[k])

    tokens = pl.ds(pl.multiple_of(core * TOK, TOK), TOK)
    mine_to = (routes.at[core], scores.at[core], raw.at[tokens], data.at[1, tokens])
    micro = ((routes_0, scores_0, fx.at[0], fg.at[0]), (routes_1, scores_1, rx.at[0], rg.at[0]))
    load_gain = load(4, gain_0, gain)
    load_gate = load(5, wg.at[0], weights.at[:, pl.ds(0, HID)])
    load_up = load(6, wu.at[0], weights.at[:, pl.ds(HID, HID)])
    for h in range(2):

        @pl.when(core == h)
        def _():
            for k in range(4):
                load(k, micro[h][k], mine_to[k]).start()

    load_gain.start()

    barrier = pltpu.get_barrier_semaphore()

    def greet(device):
        pl.semaphore_signal(barrier, inc=1, device_id=device, device_id_type=MESH)

    greet(core_mate)
    greet(x_mate)
    greet(mirror)

    @pl.when(i > 0)
    def _():
        greet(z_left)

    @pl.when(i < 3)
    def _():
        greet(z_right)

    @pl.when(i == 0)
    def _():
        for k in range(4):
            greet(at(((q + 3) % 4) * 4 + k, far_x, core, far_pipe))
        for k in (2, 3):
            greet(at(((q + 2) % 4) * 4 + k, far_x, core, far_pipe))

    @pl.when(i == 3)
    def _():
        for k in range(4):
            greet(at(((q + 1) % 4) * 4 + k, far_x, core, far_pipe))
        for k in (0, 1):
            greet(at(((q + 2) % 4) * 4 + k, far_x, core, far_pipe))

    pl.semaphore_wait(barrier, 7 + (i * (3 - i)) // 2)

    def remote(src, dst, send, recv, device):
        return pltpu.make_async_remote_copy(
            src_ref=src, dst_ref=dst, send_sem=send, recv_sem=recv, device_id=device, device_id_type=MESH
        )

    def swap(k, h):
        return remote(micro[1 - h][k], mine_to[k], swap_send.at[k], swap_recv.at[k], core_mate)

    for h in range(2):

        @pl.when(core == h)
        def _():
            for k in range(4):
                swap(k, h).start()

    load_gain.wait()
    gain_copy = remote(gain, gain_in, gain_sem.at[0], gain_sem.at[1], mirror)
    gain_copy.start()
    load_gate.start()
    load_up.start()

    def forward(slot, c, send, device):
        return remote(buf.at[slot, c], buf.at[slot, c], send, recv_sem.at[slot, c], device)

    def arrived(slot, c):
        forward(slot, c, core_sem.at[slot, 0], core_mate).wait_recv()

    def go_right(slot):
        return forward(slot, col, right_sem.at[slot], z_right)

    def go_left(slot):
        return forward(slot, col, left_sem.at[slot], z_left)

    def go_x(slot):
        return forward(slot, col, x_sem.at[slot], x_mate)

    def go_core(slot, c, which):
        return forward(slot, c, core_sem.at[slot, which], core_mate)

    far_col = far_x * 2 + core

    def first(step, zz, slot):
        return remote(
            packed.at[(q + step) % 4], buf.at[slot, far_col], first_sem.at[step],
            recv_sem.at[slot, far_col], at(zz, far_x, core, far_pipe),
        )

    own = 9 - i
    to_right = first(1, ((q + 1) % 4) * 4, 13 - i)
    to_left = first(3, ((q + 3) % 4) * 4 + 3, 5 - i)
    to_across = first(
        2, ((q + 2) % 4) * 4 + 3 * (1 - half), half * (17 - i) + (1 - half) * (1 - i)
    )
    to_mirror = first(0, z, own)
    keep = pltpu.make_async_copy(packed.at[q], buf.at[own, col], local_sem)

    def spread_own():
        @pl.when(i < 3)
        def _():
            go_right(own).start()

        @pl.when(i > 0)
        def _():
            go_left(own).start()

        go_x(own).start()
        go_core(own, col, 0).start()

    def here(k):
        load(k, micro[0][k], mine_to[k]).wait()
        swap(k, 0).wait_recv()

    here(0)
    here(1)
    main, rem = select_tables(routes, scores)
    here(2)
    values = raw[...].astype(jnp.float32)
    scale = lax.rsqrt(jnp.mean(values * values, axis=-1, keepdims=True) + 1e-06)
    gain_copy.wait_recv()
    factor = jnp.where(core == 0, gain[...], gain_in[...])
    data[0] = (values * scale * factor).astype(jnp.bfloat16)
    here(3)
    pack(main, rem, data.reshape(4 * TOK, D), packed)
    @pl.when(core == 0)
    def _():
        keep.start()
        keep.wait()
        spread_own()

    @pl.when(core == 1)
    def _():
        to_mirror.start()

    def issue(point):
        for copy, k in ((to_right, 3 - i), (to_left, i), (to_across, 4 + half * (3 - i) + (1 - half) * i)):
            due = (k <= AHEAD) if point == 0 else (k == AHEAD + point)

            @pl.when(due)
            def _():
                copy.start()

    issue(0)
    grad[...] = jnp.zeros_like(grad)

    @pl.when(core == 1)
    def _():
        arrived(own, col)
        spread_own()

    def from_left(slot):
        arrived(slot, col)

        @pl.when(i < 3)
        def _():
            go_right(slot).start()

        go_x(slot).start()
        go_core(slot, col, 0).start()

    def from_right(slot):
        arrived(slot, col)

        @pl.when(i > 0)
        def _():
            go_left(slot).start()

        go_x(slot).start()
        go_core(slot, col, 0).start()

    def from_x(slot):
        arrived(slot, xcol)
        go_core(slot, xcol, 1).start()

    def compute(base, slots, last=False):
        block = pl.ds(base, slots)
        main, rest = slots * 64, slots * 16
        for k in range(slots):
            arrived(base + k, x_lo * 2 + 1 - core)
            arrived(base + k, (1 - x_lo) * 2 + 1 - core)
        out_row, in_row = iota((main, main), 0), iota((main, main), 1)
        source = ((out_row % rest) // 4) * 16 + (out_row // rest) * 4 + out_row % 4
        turn = jnp.where(in_row == source, 1.0, 0.0).astype(jnp.bfloat16)
        tail = buf[block, :, 64:80, :].reshape(main, LANES)
        spare[:main, :] = jnp.dot(turn, tail, preferred_element_type=jnp.float32).astype(jnp.bfloat16)

        def rows_of(p):
            return jnp.concatenate(
                [
                    buf[block, :, 16 * p : 16 * p + 16, :].reshape(main, LANES),
                    spare[rest * p : rest * p + rest, :],
                ],
                axis=0,
            )

        both = jnp.zeros((main + rest, 2 * HID), jnp.float32)
        for p in range(PARTS):
            both = both + jnp.dot(
                rows_of(p), weights[p * LANES : (p + 1) * LANES, :], preferred_element_type=jnp.float32
            )
        gate, up = both[:, :HID], both[:, HID:]
        hidden = gate / (1.0 + jnp.exp(-gate)) * up
        row = iota((main + rest, HID), 0)
        moved = jnp.concatenate(
            [pltpu.roll(hidden[:main], 8, 0), pltpu.roll(hidden[main:], 2, 0)], axis=0
        )
        valid = ((row < main) & (row % 16 >= 8)) | ((row >= main) & (row % 4 >= 2))
        side = jnp.where(valid, moved, 0.0).T.astype(jnp.bfloat16)
        for p in range(PARTS):
            lanes = slice(p * LANES, (p + 1) * LANES)
            total = grad[:, lanes] + jnp.dot(side, rows_of(p), preferred_element_type=jnp.float32)
            if last:
                out_ref[0, :, lanes] = total.astype(jnp.bfloat16)
            else:
                grad[:, lanes] = total

    load_gate.wait()
    load_up.wait()
    def along_x(step):
        if step < 0:
            from_x(own)
            return

        @pl.when(step <= 5 + i)
        def _():
            from_x(own + 1 + step)

        @pl.when(step <= 8 - i)
        def _():
            from_x(own - 1 - step)

    for step in range(9):

        @pl.when(step <= 5 + i)
        def _():
            from_left(own + 1 + step)

        @pl.when(step <= 8 - i)
        def _():
            from_right(own - 1 - step)

        issue(step + 1)
        along_x(step - 1)
        if step == 4:
            compute(8 - 4 * half, 4)
        if step == 6:
            compute(4 + 4 * half, 4)
        if step == 7:
            compute(12 - 12 * half, 4)
        if step == 8:
            compute(2 + 10 * half, 2)
    along_x(8)
    compute(14 * half, 2, last=True)

    gain_copy.wait_send()
    for k in range(4):
        swap(k, 0).wait_send()
    to_right.wait_send()
    to_left.wait_send()
    to_across.wait_send()

    @pl.when(core == 1)
    def _():
        to_mirror.wait_send()

    for slot in range(16):
        go_x(slot).wait_send()
        go_core(slot, col, 0).wait_send()
        go_core(slot, xcol, 1).wait_send()
    for slot in range(16):

        @pl.when((slot >= own) & (i < 3))
        def _():
            go_right(slot).wait_send()

        @pl.when((slot <= own) & (i > 0))
        def _():
            go_left(slot).wait_send()


def body(fx, fg, rx, rg, f_routes, r_routes, f_scores, r_scores, gain, w_gate, w_up):
    vmem, hbm = pl.BlockSpec(memory_space=pltpu.VMEM), pl.BlockSpec(memory_space=pl.ANY)
    dma = pltpu.SemaphoreType.DMA
    return pl.pallas_call(
        kernel,
        name="routed_grad",
        out_shape=jax.ShapeDtypeStruct((1, HID, D), jnp.bfloat16),
        in_specs=[hbm] * 11,
        out_specs=vmem,
        scratch_shapes=[
            pltpu.VMEM((16, 4, ROWS, LANES), jnp.bfloat16),
            pltpu.VMEM((2, 8, TOK), jnp.int32),
            pltpu.VMEM((2, 8, TOK), jnp.float32),
            pltpu.VMEM((1, D), jnp.float32),
            pltpu.VMEM((1, D), jnp.float32),
            pltpu.VMEM((2 * TOK, D), jnp.bfloat16),
            pltpu.VMEM((2, 2 * TOK, D), jnp.bfloat16),
            pltpu.VMEM((4, ROWS, LANES), jnp.bfloat16),
            pltpu.VMEM((D, 2 * HID), jnp.bfloat16),
            pltpu.VMEM((256, LANES), jnp.bfloat16),
            pltpu.VMEM((HID, D), jnp.float32),
            dma((7,)), dma, dma((2,)), dma((4,)), dma((4,)), dma((4,)), dma((16,)), dma((16,)), dma((16,)),
            dma((16, 2)), dma((16, 4)),
        ],
        compiler_params=pltpu.CompilerParams(
            collective_id=0, has_side_effects=True, vmem_limit_bytes=63 << 20
        ),
        cost_estimate=pl.CostEstimate(flops=6 << 30, bytes_accessed=5 << 20, transcendentals=1 << 17),
    )(
        fx, fg, rx, rg, f_routes[0].T, r_routes[0].T, f_scores[0].T, r_scores[0].T, gain, w_gate, w_up
    )


def solution(mesh):
    rows = P("pipe", "expert", None)
    in_specs = (rows,) * 8 + (P("pipe", None),) + (P("pipe", None, "expert"),) * 2
    return jax.shard_map(body, mesh=mesh, in_specs=in_specs, out_specs=rows, check_vma=False)
```

```python
import functools

import jax
import jax.numpy as jnp
from jax import lax
from jax.experimental import pallas as pl
from jax.experimental.pallas import tpu as pltpu
from jax.sharding import PartitionSpec as P

MESH = pl.DeviceIdType.MESH
AHEAD = 1
D = 3584
TOK = 64
CAP = 5
PARTS = 4
LANES = D // PARTS
ROWS = 80
PIECES = ((0, 48), (48, 32))
HID = 128


def iota(shape, axis):
    return lax.broadcasted_iota(jnp.int32, shape, axis)


def select_tables(routes_ref, scores_ref):
    place = jnp.zeros((8, 4 * TOK), jnp.float32)
    weight = jnp.zeros((8, 4 * TOK), jnp.float32)
    row = iota((8, TOK), 0)
    token, lane = iota((TOK, 4 * TOK), 0), iota((TOK, 4 * TOK), 1)
    for h in range(2):
        routes, scores = routes_ref[h], scores_ref[h]
        share = 2.5 * scores / jnp.sum(scores, axis=0, keepdims=True)
        coef = jnp.zeros((8, TOK), jnp.float32)
        for e in range(4):
            mine = jnp.sum(jnp.where(routes == e, share, 0.0), axis=0, keepdims=True)
            coef = coef + jnp.where(row == e, mine, 0.0)
        coef = coef.astype(jnp.bfloat16)
        taken = jnp.where(coef.astype(jnp.float32) > 0, 1.0, 0.0).astype(jnp.bfloat16)
        here = (lane // TOK) % 2 == h
        upto = jnp.where(here & (token <= lane % TOK), 1.0, 0.0).astype(jnp.bfloat16)
        same = jnp.where(here & (token == lane % TOK), 1.0, 0.0).astype(jnp.bfloat16)
        place = place + jnp.dot(taken, upto, preferred_element_type=jnp.float32)
        weight = weight + jnp.dot(coef, same, preferred_element_type=jnp.float32)
    lane = iota((8, 4 * TOK), 1)
    place = place + jnp.where((lane // TOK) % 2 == 1, CAP - 1.0, -1.0)
    r, lane = iota((16, 4 * TOK), 0), iota((16, 4 * TOK), 1)
    left = lane < 2 * TOK
    main_ok = left == (r < 8)
    main_slot = (r % 8).astype(jnp.float32)
    rem_ok = left == (r % 4 < 2)
    rem_slot = (8 + r % 2).astype(jnp.float32)
    main, rem = [], []
    for e in range(4):
        where = jnp.broadcast_to(place[e : e + 1], (16, 4 * TOK))
        much = jnp.broadcast_to(weight[e : e + 1], (16, 4 * TOK))
        value = jnp.where(much > 0, jnp.where(left, 1.0, much), 0.0)
        main.append(jnp.where(main_ok & (where == main_slot), value, 0.0))
        rem.append(jnp.where(rem_ok & (where == rem_slot), value, 0.0))
    return jnp.concatenate(main, axis=0), jnp.concatenate(rem, axis=0)


def pack(main, rem, data, packed):
    part = (iota((64, 4 * TOK), 0) % 16) // 4
    total = jnp.zeros((64, LANES), jnp.float32)
    for p in range(PARTS):
        lhs = jnp.concatenate([main, jnp.where(part == p, rem, 0.0)], axis=0).astype(jnp.bfloat16)
        rows = jnp.dot(
            lhs, data[:, p * LANES : (p + 1) * LANES], preferred_element_type=jnp.float32
        )
        packed[:, 16 * p : 16 * p + 16, :] = rows[:64].astype(jnp.bfloat16).reshape(4, 16, LANES)
        total = total + rows[64:]
    packed[:, 64:80, :] = total.astype(jnp.bfloat16).reshape(4, 16, LANES)


def kernel(
    fx, fg, rx, rg, routes_0, routes_1, scores_0, scores_1, gain_0, wg, wu, out_ref,
    buf, routes, scores, gain, gain_out, gain_in, raw, data, packed, weights, spare, grad,
    load_sem, local_sem, gain_sem, swap_send, swap_recv, first_sem, right_sem, left_sem, x_sem, core_sem, recv_sem,
):
    pipe = lax.axis_index("pipe")
    me = lax.axis_index("expert")
    z, x_lo, core = me // 4, (me // 2) % 2, me % 2
    q, i = z // 4, z % 4
    col = x_lo * 2 + core
    xcol = (1 - x_lo) * 2 + core
    half = i // 2

    def at(zz, xx, cc, pp=None):
        return (pipe if pp is None else pp, zz * 4 + xx * 2 + cc)

    far_pipe = pipe * (1 - core) + (lax.axis_size("pipe") - 1 - pipe) * core
    far_x = x_lo * (1 - core) + (1 - x_lo) * core
    mirror = at(z, 1 - x_lo, core, lax.axis_size("pipe") - 1 - pipe)
    core_mate = at(z, x_lo, 1 - core)
    x_mate = at(z, 1 - x_lo, core)
    z_right = at((z + 1) % 16, x_lo, core)
    z_left = at((z + 15) % 16, x_lo, core)

    def load(k, source, target):
        return pltpu.make_async_copy(source, target, load_sem.at[k])

    tokens = pl.ds(pl.multiple_of(core * TOK, TOK), TOK)
    mine_to = (routes.at[core], scores.at[core], raw.at[tokens], data.at[1, tokens])
    micro = ((routes_0, scores_0, fx.at[0], fg.at[0]), (routes_1, scores_1, rx.at[0], rg.at[0]))
    load_gain = load(4, gain_0, gain)
    load_gate = load(5, wg.at[0], weights.at[:, pl.ds(0, HID)])
    load_up = load(6, wu.at[0], weights.at[:, pl.ds(HID, HID)])
    for h in range(2):

        @pl.when(core == h)
        def _():
            for k in range(4):
                load(k, micro[h][k], mine_to[k]).start()

    load_gain.start()

    barrier = pltpu.get_barrier_semaphore()

    def greet(device):
        pl.semaphore_signal(barrier, inc=1, device_id=device, device_id_type=MESH)

    greet(core_mate)
    greet(x_mate)
    greet(mirror)

    @pl.when(i > 0)
    def _():
        greet(z_left)

    @pl.when(i < 3)
    def _():
        greet(z_right)

    @pl.when(i == 0)
    def _():
        for k in range(4):
            greet(at(((q + 3) % 4) * 4 + k, far_x, core, far_pipe))
        for k in (2, 3):
            greet(at(((q + 2) % 4) * 4 + k, far_x, core, far_pipe))

    @pl.when(i == 3)
    def _():
        for k in range(4):
            greet(at(((q + 1) % 4) * 4 + k, far_x, core, far_pipe))
        for k in (0, 1):
            greet(at(((q + 2) % 4) * 4 + k, far_x, core, far_pipe))

    pl.semaphore_wait(barrier, 7 + (i * (3 - i)) // 2)

    def remote(src, dst, send, recv, device):
        return pltpu.make_async_remote_copy(
            src_ref=src, dst_ref=dst, send_sem=send, recv_sem=recv, device_id=device, device_id_type=MESH
        )

    def swap(k, h):
        return remote(micro[1 - h][k], mine_to[k], swap_send.at[k], swap_recv.at[k], core_mate)

    for h in range(2):

        @pl.when(core == h)
        def _():
            for k in range(4):
                swap(k, h).start()

    load_gain.wait()
    gain_out[...] = gain[...]
    gain_copy = remote(gain_out, gain_in, gain_sem.at[0], gain_sem.at[1], mirror)
    gain_copy.start()
    load_gate.start()
    load_up.start()

    def piece(slot, c, h):
        return buf.at[slot, c, pl.ds(*PIECES[h])]

    def forward(slot, c, h, send, device):
        here = piece(slot, c, h)
        return remote(here, here, send, recv_sem.at[slot, c, h], device)

    def arrived(slot, c, h):
        forward(slot, c, h, core_sem.at[slot, 0], core_mate).wait_recv()

    def go_right(slot, h):
        return forward(slot, col, h, right_sem.at[slot, h], z_right)

    def go_left(slot, h):
        return forward(slot, col, h, left_sem.at[slot, h], z_left)

    def go_x(slot, h):
        return forward(slot, col, h, x_sem.at[slot, h], x_mate)

    def go_core(slot, c, which):
        whole = buf.at[slot, c]
        return remote(whole, whole, core_sem.at[slot, which], recv_sem.at[slot, c, 0], core_mate)

    def from_core(slot, c):
        go_core(slot, c, 0).wait_recv()

    far_col = far_x * 2 + core

    def first(step, zz, slot):
        return [
            remote(
                packed.at[(q + step) % 4, pl.ds(*PIECES[h])], buf.at[slot, far_col, pl.ds(*PIECES[h])],
                first_sem.at[step, h], recv_sem.at[slot, far_col, h], at(zz, far_x, core, far_pipe),
            )
            for h in range(2)
        ]

    own = 9 - i
    to_right = first(1, ((q + 1) % 4) * 4, 13 - i)
    to_left = first(3, ((q + 3) % 4) * 4 + 3, 5 - i)
    to_across = first(
        2, ((q + 2) % 4) * 4 + 3 * (1 - half), half * (17 - i) + (1 - half) * (1 - i)
    )
    to_mirror = first(0, z, own)
    keep = pltpu.make_async_copy(packed.at[q], buf.at[own, col], local_sem)

    def spread_own(h):
        @pl.when(i < 3)
        def _():
            go_right(own, h).start()

        @pl.when(i > 0)
        def _():
            go_left(own, h).start()

        go_x(own, h).start()
        if h == 1:
            go_core(own, col, 0).start()

    def here(k):
        load(k, micro[0][k], mine_to[k]).wait()
        swap(k, 0).wait_recv()

    here(0)
    here(1)
    main, rem = select_tables(routes, scores)
    here(2)
    values = raw[...].astype(jnp.float32)
    scale = lax.rsqrt(jnp.mean(values * values, axis=-1, keepdims=True) + 1e-06)

    @pl.when(core == 1)
    def _():
        gain_copy.wait_recv()
        gain[...] = gain_in[...]

    factor = gain[...]
    data[0] = (values * scale * factor).astype(jnp.bfloat16)
    here(3)
    pack(main, rem, data.reshape(4 * TOK, D), packed)
    @pl.when(core == 0)
    def _():
        keep.start()
        keep.wait()
        spread_own(0)
        spread_own(1)

    @pl.when(core == 1)
    def _():
        for copy in to_mirror:
            copy.start()

    def issue(point):
        for copies, k in ((to_right, 3 - i), (to_left, i), (to_across, 4 + half * (3 - i) + (1 - half) * i)):
            due = (k <= AHEAD) if point == 0 else (k == AHEAD + point)

            @pl.when(due)
            def _():
                for copy in copies:
                    copy.start()

    issue(0)
    grad[...] = jnp.zeros_like(grad)

    @pl.when(core == 1)
    def _():
        for h in range(2):
            arrived(own, col, h)
            spread_own(h)

    def from_left(slot, h):
        arrived(slot, col, h)

        @pl.when(i < 3)
        def _():
            go_right(slot, h).start()

        go_x(slot, h).start()
        if h == 1:
            go_core(slot, col, 0).start()

    def from_right(slot, h):
        arrived(slot, col, h)

        @pl.when(i > 0)
        def _():
            go_left(slot, h).start()

        go_x(slot, h).start()
        if h == 1:
            go_core(slot, col, 0).start()

    def from_x(slot):
        arrived(slot, xcol, 0)
        arrived(slot, xcol, 1)
        go_core(slot, xcol, 1).start()

    def compute(base, slots, last=False):
        block = pl.ds(base, slots)
        main, rest = slots * 64, slots * 16
        for k in range(slots):
            from_core(base + k, x_lo * 2 + 1 - core)
            from_core(base + k, (1 - x_lo) * 2 + 1 - core)
        out_row, in_row = iota((main, main), 0), iota((main, main), 1)
        source = ((out_row % rest) // 4) * 16 + (out_row // rest) * 4 + out_row % 4
        turn = jnp.where(in_row == source, 1.0, 0.0).astype(jnp.bfloat16)
        tail = buf[block, :, 64:80, :].reshape(main, LANES)
        spare[:main, :] = jnp.dot(turn, tail, preferred_element_type=jnp.float32).astype(jnp.bfloat16)

        def rows_of(p):
            return jnp.concatenate(
                [
                    buf[block, :, 16 * p : 16 * p + 16, :].reshape(main, LANES),
                    spare[rest * p : rest * p + rest, :],
                ],
                axis=0,
            )

        both = jnp.zeros((main + rest, 2 * HID), jnp.float32)
        for p in range(PARTS):
            both = both + jnp.dot(
                rows_of(p), weights[p * LANES : (p + 1) * LANES, :], preferred_element_type=jnp.float32
            )
        gate, up = both[:, :HID], both[:, HID:]
        hidden = gate / (1.0 + jnp.exp(-gate)) * up
        row = iota((main + rest, HID), 0)
        moved = jnp.concatenate(
            [pltpu.roll(hidden[:main], 8, 0), pltpu.roll(hidden[main:], 2, 0)], axis=0
        )
        valid = ((row < main) & (row % 16 >= 8)) | ((row >= main) & (row % 4 >= 2))
        side = jnp.where(valid, moved, 0.0).T.astype(jnp.bfloat16)
        for p in range(PARTS):
            lanes = slice(p * LANES, (p + 1) * LANES)
            total = grad[:, lanes] + jnp.dot(side, rows_of(p), preferred_element_type=jnp.float32)
            if last:
                out_ref[0, :, lanes] = total.astype(jnp.bfloat16)
            else:
                grad[:, lanes] = total

    load_gate.wait()
    load_up.wait()
    def along_x(step):
        if step < 0:
            from_x(own)
            return

        @pl.when(step <= 5 + i)
        def _():
            from_x(own + 1 + step)

        @pl.when(step <= 8 - i)
        def _():
            from_x(own - 1 - step)

    for step in range(9):

        for h in range(2):

            @pl.when(step <= 5 + i)
            def _():
                from_left(own + 1 + step, h)

            @pl.when(step <= 8 - i)
            def _():
                from_right(own - 1 - step, h)

        issue(step + 1)
        along_x(step - 1)
        if step == 4:
            compute(8 - 4 * half, 4)
        if step == 6:
            compute(4 + 4 * half, 4)
        if step == 7:
            compute(12 - 12 * half, 4)
        if step == 8:
            compute(2 + 10 * half, 2)
    along_x(8)
    compute(14 * half, 2, last=True)

    @pl.when(core == 0)
    def _():
        gain_copy.wait_recv()

    gain_copy.wait_send()
    for k in range(4):
        swap(k, 0).wait_send()
    for copy in to_right + to_left + to_across:
        copy.wait_send()

    @pl.when(core == 1)
    def _():
        for copy in to_mirror:
            copy.wait_send()

    for slot in range(16):
        go_core(slot, col, 0).wait_send()
        go_core(slot, xcol, 1).wait_send()
        for h in range(2):
            go_x(slot, h).wait_send()

        @pl.when((slot >= own) & (i < 3))
        def _():
            for h in range(2):
                go_right(slot, h).wait_send()

        @pl.when((slot <= own) & (i > 0))
        def _():
            for h in range(2):
                go_left(slot, h).wait_send()


def body(fx, fg, rx, rg, f_routes, r_routes, f_scores, r_scores, gain, w_gate, w_up):
    vmem, hbm = pl.BlockSpec(memory_space=pltpu.VMEM), pl.BlockSpec(memory_space=pl.ANY)
    dma = pltpu.SemaphoreType.DMA
    return pl.pallas_call(
        kernel,
        name="routed_grad",
        out_shape=pltpu.VMEM((1, HID, D), jnp.bfloat16),
        in_specs=[hbm] * 11,
        out_specs=vmem,
        scratch_shapes=[
            pltpu.VMEM((16, 4, ROWS, LANES), jnp.bfloat16),
            pltpu.VMEM((2, 8, TOK), jnp.int32),
            pltpu.VMEM((2, 8, TOK), jnp.float32),
            pltpu.VMEM((1, D), jnp.float32),
            pltpu.VMEM((1, D), jnp.float32),
            pltpu.VMEM((1, D), jnp.float32),
            pltpu.VMEM((2 * TOK, D), jnp.bfloat16),
            pltpu.VMEM((2, 2 * TOK, D), jnp.bfloat16),
            pltpu.VMEM((4, ROWS, LANES), jnp.bfloat16),
            pltpu.VMEM((D, 2 * HID), jnp.bfloat16),
            pltpu.VMEM((256, LANES), jnp.bfloat16),
            pltpu.VMEM((HID, D), jnp.float32),
            dma((7,)), dma, dma((2,)), dma((4,)), dma((4,)), dma((4, 2)), dma((16, 2)), dma((16, 2)), dma((16, 2)),
            dma((16, 2)), dma((16, 4, 2)),
        ],
        compiler_params=pltpu.CompilerParams(
            collective_id=0, has_side_effects=True, vmem_limit_bytes=63 << 20
        ),
        cost_estimate=pl.CostEstimate(flops=6 << 30, bytes_accessed=5 << 20, transcendentals=1 << 17),
    )(
        fx, fg, rx, rg, f_routes[0].T, r_routes[0].T, f_scores[0].T, r_scores[0].T, gain, w_gate, w_up
    )


def solution(mesh):
    rows = P("pipe", "expert", None)
    in_specs = (rows,) * 8 + (P("pipe", None),) + (P("pipe", None, "expert"),) * 2
    return jax.shard_map(body, mesh=mesh, in_specs=in_specs, out_specs=rows, check_vma=False)
```

```python
import functools

import jax
import jax.numpy as jnp
from jax import lax
from jax.experimental import pallas as pl
from jax.experimental.pallas import tpu as pltpu
from jax.sharding import PartitionSpec as P

MESH = pl.DeviceIdType.MESH
AHEAD = 1
D = 3584
TOK = 64
CAP = 5
PARTS = 4
LANES = D // PARTS
ROWS = 80
PIECES = ((0, 48), (48, 32))
HID = 128


def iota(shape, axis):
    return lax.broadcasted_iota(jnp.int32, shape, axis)


def select_tables(routes_ref, scores_ref):
    place = jnp.zeros((8, 4 * TOK), jnp.float32)
    weight = jnp.zeros((8, 4 * TOK), jnp.float32)
    row = iota((8, TOK), 0)
    token, lane = iota((TOK, 4 * TOK), 0), iota((TOK, 4 * TOK), 1)
    for h in range(2):
        routes, scores = routes_ref[h], scores_ref[h]
        share = 2.5 * scores / jnp.sum(scores, axis=0, keepdims=True)
        coef = jnp.zeros((8, TOK), jnp.float32)
        for e in range(4):
            mine = jnp.sum(jnp.where(routes == e, share, 0.0), axis=0, keepdims=True)
            coef = coef + jnp.where(row == e, mine, 0.0)
        coef = coef.astype(jnp.bfloat16)
        taken = jnp.where(coef.astype(jnp.float32) > 0, 1.0, 0.0).astype(jnp.bfloat16)
        here = (lane // TOK) % 2 == h
        upto = jnp.where(here & (token <= lane % TOK), 1.0, 0.0).astype(jnp.bfloat16)
        same = jnp.where(here & (token == lane % TOK), 1.0, 0.0).astype(jnp.bfloat16)
        place = place + jnp.dot(taken, upto, preferred_element_type=jnp.float32)
        weight = weight + jnp.dot(coef, same, preferred_element_type=jnp.float32)
    lane = iota((8, 4 * TOK), 1)
    place = place + jnp.where((lane // TOK) % 2 == 1, CAP - 1.0, -1.0)
    r, lane = iota((16, 4 * TOK), 0), iota((16, 4 * TOK), 1)
    left = lane < 2 * TOK
    main_ok = left == (r < 8)
    main_slot = (r % 8).astype(jnp.float32)
    rem_ok = left == (r % 4 < 2)
    rem_slot = (8 + r % 2).astype(jnp.float32)
    main, rem = [], []
    for e in range(4):
        where = jnp.broadcast_to(place[e : e + 1], (16, 4 * TOK))
        much = jnp.broadcast_to(weight[e : e + 1], (16, 4 * TOK))
        value = jnp.where(much > 0, jnp.where(left, 1.0, much), 0.0)
        main.append(jnp.where(main_ok & (where == main_slot), value, 0.0))
        rem.append(jnp.where(rem_ok & (where == rem_slot), value, 0.0))
    return jnp.concatenate(main, axis=0), jnp.concatenate(rem, axis=0)


def pack(main, rem, data, packed):
    part = (iota((64, 4 * TOK), 0) % 16) // 4
    total = jnp.zeros((64, LANES), jnp.float32)
    for p in range(PARTS):
        lhs = jnp.concatenate([main, jnp.where(part == p, rem, 0.0)], axis=0).astype(jnp.bfloat16)
        rows = jnp.dot(
            lhs, data[:, p * LANES : (p + 1) * LANES], preferred_element_type=jnp.float32
        )
        packed[:, 16 * p : 16 * p + 16, :] = rows[:64].astype(jnp.bfloat16).reshape(4, 16, LANES)
        total = total + rows[64:]
    packed[:, 64:80, :] = total.astype(jnp.bfloat16).reshape(4, 16, LANES)


def kernel(
    fx, fg, rx, rg, routes_0, routes_1, scores_0, scores_1, gain_0, wg, wu, out_ref,
    buf, routes, scores, gain, gain_out, gain_in, raw, data, packed, weights, spare, grad,
    load_sem, local_sem, gain_sem, swap_send, swap_recv, first_sem, right_sem, left_sem, x_sem, core_sem, recv_sem,
):
    pipe = lax.axis_index("pipe")
    me = lax.axis_index("expert")
    z, x_lo, core = me // 4, (me // 2) % 2, me % 2
    q, i = z // 4, z % 4
    col = x_lo * 2 + core
    xcol = (1 - x_lo) * 2 + core
    half = i // 2

    def at(zz, xx, cc, pp=None):
        return (pipe if pp is None else pp, zz * 4 + xx * 2 + cc)

    far_pipe = pipe * (1 - core) + (lax.axis_size("pipe") - 1 - pipe) * core
    far_x = x_lo * (1 - core) + (1 - x_lo) * core
    mirror = at(z, 1 - x_lo, core, lax.axis_size("pipe") - 1 - pipe)
    core_mate = at(z, x_lo, 1 - core)
    x_mate = at(z, 1 - x_lo, core)
    z_right = at((z + 1) % 16, x_lo, core)
    z_left = at((z + 15) % 16, x_lo, core)

    barrier = pltpu.get_barrier_semaphore()

    def greet(device):
        pl.semaphore_signal(barrier, inc=1, device_id=device, device_id_type=MESH)

    greet(core_mate)
    greet(x_mate)
    greet(mirror)

    @pl.when(i > 0)
    def _():
        greet(z_left)

    @pl.when(i < 3)
    def _():
        greet(z_right)

    @pl.when(i == 0)
    def _():
        for k in range(4):
            greet(at(((q + 3) % 4) * 4 + k, far_x, core, far_pipe))
        for k in (2, 3):
            greet(at(((q + 2) % 4) * 4 + k, far_x, core, far_pipe))

    @pl.when(i == 3)
    def _():
        for k in range(4):
            greet(at(((q + 1) % 4) * 4 + k, far_x, core, far_pipe))
        for k in (0, 1):
            greet(at(((q + 2) % 4) * 4 + k, far_x, core, far_pipe))

    def load(k, source, target):
        return pltpu.make_async_copy(source, target, load_sem.at[k])

    tokens = pl.ds(pl.multiple_of(core * TOK, TOK), TOK)
    mine_to = (routes.at[core], scores.at[core], raw.at[tokens], data.at[1, tokens])
    micro = ((routes_0, scores_0, fx.at[0], fg.at[0]), (routes_1, scores_1, rx.at[0], rg.at[0]))
    load_gain = load(4, gain_0, gain)
    load_gate = load(5, wg.at[0], weights.at[:, pl.ds(0, HID)])
    load_up = load(6, wu.at[0], weights.at[:, pl.ds(HID, HID)])
    for h in range(2):

        @pl.when(core == h)
        def _():
            for k in range(4):
                load(k, micro[h][k], mine_to[k]).start()

    load_gain.start()

    pl.semaphore_wait(barrier, 7 + (i * (3 - i)) // 2)

    def remote(src, dst, send, recv, device):
        return pltpu.make_async_remote_copy(
            src_ref=src, dst_ref=dst, send_sem=send, recv_sem=recv, device_id=device, device_id_type=MESH
        )

    def swap(k, h):
        return remote(micro[1 - h][k], mine_to[k], swap_send.at[k], swap_recv.at[k], core_mate)

    for h in range(2):

        @pl.when(core == h)
        def _():
            for k in range(4):
                swap(k, h).start()

    load_gain.wait()
    gain_out[...] = gain[...]
    gain_copy = remote(gain_out, gain_in, gain_sem.at[0], gain_sem.at[1], mirror)
    gain_copy.start()
    load_gate.start()
    load_up.start()

    def piece(slot, c, h):
        return buf.at[slot, c, pl.ds(*PIECES[h])]

    def forward(slot, c, h, send, device):
        here = piece(slot, c, h)
        return remote(here, here, send, recv_sem.at[slot, c, h], device)

    def arrived(slot, c, h):
        forward(slot, c, h, core_sem.at[slot, 0], core_mate).wait_recv()

    def go_right(slot, h):
        return forward(slot, col, h, right_sem.at[slot, h], z_right)

    def go_left(slot, h):
        return forward(slot, col, h, left_sem.at[slot, h], z_left)

    def go_x(slot, h):
        return forward(slot, col, h, x_sem.at[slot, h], x_mate)

    def go_core(slot, c, which):
        whole = buf.at[slot, c]
        return remote(whole, whole, core_sem.at[slot, which], recv_sem.at[slot, c, 0], core_mate)

    def from_core(slot, c):
        go_core(slot, c, 0).wait_recv()

    far_col = far_x * 2 + core

    def first(step, zz, slot):
        return [
            remote(
                packed.at[(q + step) % 4, pl.ds(*PIECES[h])], buf.at[slot, far_col, pl.ds(*PIECES[h])],
                first_sem.at[step, h], recv_sem.at[slot, far_col, h], at(zz, far_x, core, far_pipe),
            )
            for h in range(2)
        ]

    own = 9 - i
    to_right = first(1, ((q + 1) % 4) * 4, 13 - i)
    to_left = first(3, ((q + 3) % 4) * 4 + 3, 5 - i)
    to_across = first(
        2, ((q + 2) % 4) * 4 + 3 * (1 - half), half * (17 - i) + (1 - half) * (1 - i)
    )
    to_mirror = first(0, z, own)
    keep = pltpu.make_async_copy(packed.at[q], buf.at[own, col], local_sem)

    def spread_own(h):
        @pl.when(i < 3)
        def _():
            go_right(own, h).start()

        @pl.when(i > 0)
        def _():
            go_left(own, h).start()

        go_x(own, h).start()
        if h == 1:
            go_core(own, col, 0).start()

    def here(k):
        load(k, micro[0][k], mine_to[k]).wait()
        swap(k, 0).wait_recv()

    here(0)
    here(1)
    main, rem = select_tables(routes, scores)
    here(2)
    values = raw[...].astype(jnp.float32)
    scale = lax.rsqrt(jnp.mean(values * values, axis=-1, keepdims=True) + 1e-06)

    @pl.when(core == 1)
    def _():
        gain_copy.wait_recv()
        gain[...] = gain_in[...]

    factor = gain[...]
    data[0] = (values * scale * factor).astype(jnp.bfloat16)
    here(3)
    pack(main, rem, data.reshape(4 * TOK, D), packed)
    @pl.when(core == 0)
    def _():
        keep.start()
        keep.wait()
        spread_own(0)
        spread_own(1)

    @pl.when(core == 1)
    def _():
        for copy in to_mirror:
            copy.start()

    def issue(point):
        for copies, k in ((to_right, 3 - i), (to_left, i), (to_across, 4 + half * (3 - i) + (1 - half) * i)):
            due = (k <= AHEAD) if point == 0 else (k == AHEAD + point)

            @pl.when(due)
            def _():
                for copy in copies:
                    copy.start()

    issue(0)
    grad[...] = jnp.zeros_like(grad)

    @pl.when(core == 1)
    def _():
        for h in range(2):
            arrived(own, col, h)
            spread_own(h)

    def from_left(slot, h):
        arrived(slot, col, h)

        @pl.when(i < 3)
        def _():
            go_right(slot, h).start()

        go_x(slot, h).start()
        if h == 1:
            go_core(slot, col, 0).start()

    def from_right(slot, h):
        arrived(slot, col, h)

        @pl.when(i > 0)
        def _():
            go_left(slot, h).start()

        go_x(slot, h).start()
        if h == 1:
            go_core(slot, col, 0).start()

    def from_x(slot):
        arrived(slot, xcol, 0)
        arrived(slot, xcol, 1)
        go_core(slot, xcol, 1).start()

    def compute(base, slots, last=False):
        block = pl.ds(base, slots)
        main, rest = slots * 64, slots * 16
        for k in range(slots):
            from_core(base + k, x_lo * 2 + 1 - core)
            from_core(base + k, (1 - x_lo) * 2 + 1 - core)
        out_row, in_row = iota((main, main), 0), iota((main, main), 1)
        source = ((out_row % rest) // 4) * 16 + (out_row // rest) * 4 + out_row % 4
        turn = jnp.where(in_row == source, 1.0, 0.0).astype(jnp.bfloat16)
        tail = buf[block, :, 64:80, :].reshape(main, LANES)
        spare[:main, :] = jnp.dot(turn, tail, preferred_element_type=jnp.float32).astype(jnp.bfloat16)

        def main_of(p):
            return buf[block, :, 16 * p : 16 * p + 16, :].reshape(main, LANES)

        def rest_of(p):
            return spare[rest * p : rest * p + rest, :]

        both = []
        for size, rows_of in ((main, main_of), (rest, rest_of)):
            total = jnp.zeros((size, 2 * HID), jnp.float32)
            for p in range(PARTS):
                lanes = slice(p * LANES, (p + 1) * LANES)
                total = total + jnp.dot(rows_of(p), weights[lanes, :], preferred_element_type=jnp.float32)
            both.append(total)
        both = jnp.concatenate(both, axis=0)
        gate, up = both[:, :HID], both[:, HID:]
        hidden = gate / (1.0 + jnp.exp(-gate)) * up
        row = iota((main + rest, HID), 0)
        moved = jnp.concatenate(
            [pltpu.roll(hidden[:main], 8, 0), pltpu.roll(hidden[main:], 2, 0)], axis=0
        )
        valid = ((row < main) & (row % 16 >= 8)) | ((row >= main) & (row % 4 >= 2))
        side = jnp.where(valid, moved, 0.0).T.astype(jnp.bfloat16)
        for p in range(PARTS):
            lanes = slice(p * LANES, (p + 1) * LANES)
            total = grad[:, lanes] + jnp.dot(
                side[:, :main], main_of(p), preferred_element_type=jnp.float32
            )
            total = total + jnp.dot(side[:, main:], rest_of(p), preferred_element_type=jnp.float32)
            if last:
                out_ref[0, :, lanes] = total.astype(jnp.bfloat16)
            else:
                grad[:, lanes] = total

    load_gate.wait()
    load_up.wait()
    def along_x(step):
        if step < 0:
            from_x(own)
            return

        @pl.when(step <= 5 + i)
        def _():
            from_x(own + 1 + step)

        @pl.when(step <= 8 - i)
        def _():
            from_x(own - 1 - step)

    for step in range(9):

        for h in range(2):

            @pl.when(step <= 5 + i)
            def _():
                from_left(own + 1 + step, h)

            @pl.when(step <= 8 - i)
            def _():
                from_right(own - 1 - step, h)

        issue(step + 1)
        along_x(step - 1)
        if step == 4:
            compute(8 - 4 * half, 4)
        if step == 6:
            compute(4 + 4 * half, 4)
        if step == 7:
            compute(12 - 12 * half, 4)
        if step == 8:
            compute(2 + 10 * half, 2)
    along_x(8)
    compute(14 * half, 2, last=True)

    @pl.when(core == 0)
    def _():
        gain_copy.wait_recv()

    gain_copy.wait_send()
    for k in range(4):
        swap(k, 0).wait_send()
    for copy in to_right + to_left + to_across:
        copy.wait_send()

    @pl.when(core == 1)
    def _():
        for copy in to_mirror:
            copy.wait_send()

    for slot in range(16):
        go_core(slot, col, 0).wait_send()
        go_core(slot, xcol, 1).wait_send()
        for h in range(2):
            go_x(slot, h).wait_send()

        @pl.when((slot >= own) & (i < 3))
        def _():
            for h in range(2):
                go_right(slot, h).wait_send()

        @pl.when((slot <= own) & (i > 0))
        def _():
            for h in range(2):
                go_left(slot, h).wait_send()


def body(fx, fg, rx, rg, f_routes, r_routes, f_scores, r_scores, gain, w_gate, w_up):
    vmem, hbm = pl.BlockSpec(memory_space=pltpu.VMEM), pl.BlockSpec(memory_space=pl.ANY)
    dma = pltpu.SemaphoreType.DMA
    return pl.pallas_call(
        kernel,
        name="routed_grad",
        out_shape=pltpu.VMEM((1, HID, D), jnp.bfloat16),
        in_specs=[hbm] * 11,
        out_specs=vmem,
        scratch_shapes=[
            pltpu.VMEM((16, 4, ROWS, LANES), jnp.bfloat16),
            pltpu.VMEM((2, 8, TOK), jnp.int32),
            pltpu.VMEM((2, 8, TOK), jnp.float32),
            pltpu.VMEM((1, D), jnp.float32),
            pltpu.VMEM((1, D), jnp.float32),
            pltpu.VMEM((1, D), jnp.float32),
            pltpu.VMEM((2 * TOK, D), jnp.bfloat16),
            pltpu.VMEM((2, 2 * TOK, D), jnp.bfloat16),
            pltpu.VMEM((4, ROWS, LANES), jnp.bfloat16),
            pltpu.VMEM((D, 2 * HID), jnp.bfloat16),
            pltpu.VMEM((256, LANES), jnp.bfloat16),
            pltpu.VMEM((HID, D), jnp.float32),
            dma((7,)), dma, dma((2,)), dma((4,)), dma((4,)), dma((4, 2)), dma((16, 2)), dma((16, 2)), dma((16, 2)),
            dma((16, 2)), dma((16, 4, 2)),
        ],
        compiler_params=pltpu.CompilerParams(
            collective_id=0, has_side_effects=True, vmem_limit_bytes=63 << 20
        ),
        cost_estimate=pl.CostEstimate(flops=6 << 30, bytes_accessed=5 << 20, transcendentals=1 << 17),
    )(
        fx, fg, rx, rg, f_routes[0].T, r_routes[0].T, f_scores[0].T, r_scores[0].T, gain, w_gate, w_up
    )


def solution(mesh):
    rows = P("pipe", "expert", None)
    in_specs = (rows,) * 8 + (P("pipe", None),) + (P("pipe", None, "expert"),) * 2
    return jax.shard_map(body, mesh=mesh, in_specs=in_specs, out_specs=rows, check_vma=False)
```

```python
import functools

import jax
import jax.numpy as jnp
from jax import lax
from jax.experimental import pallas as pl
from jax.experimental.pallas import tpu as pltpu
from jax.sharding import PartitionSpec as P

MESH = pl.DeviceIdType.MESH
AHEAD = 1
D = 3584
TOK = 64
CAP = 5
PARTS = 4
LANES = D // PARTS
ROWS = 80
PIECES = ((0, 48), (48, 32))
HID = 128


def iota(shape, axis):
    return lax.broadcasted_iota(jnp.int32, shape, axis)


def select_tables(routes_ref, scores_ref):
    place = jnp.zeros((8, 4 * TOK), jnp.float32)
    weight = jnp.zeros((8, 4 * TOK), jnp.float32)
    row = iota((8, TOK), 0)
    token, lane = iota((TOK, 4 * TOK), 0), iota((TOK, 4 * TOK), 1)
    for h in range(2):
        routes, scores = routes_ref[h], scores_ref[h]
        share = 2.5 * scores / jnp.sum(scores, axis=0, keepdims=True)
        coef = jnp.zeros((8, TOK), jnp.float32)
        for e in range(4):
            mine = jnp.sum(jnp.where(routes == e, share, 0.0), axis=0, keepdims=True)
            coef = coef + jnp.where(row == e, mine, 0.0)
        coef = coef.astype(jnp.bfloat16)
        taken = jnp.where(coef.astype(jnp.float32) > 0, 1.0, 0.0).astype(jnp.bfloat16)
        here = (lane // TOK) % 2 == h
        upto = jnp.where(here & (token <= lane % TOK), 1.0, 0.0).astype(jnp.bfloat16)
        same = jnp.where(here & (token == lane % TOK), 1.0, 0.0).astype(jnp.bfloat16)
        place = place + jnp.dot(taken, upto, preferred_element_type=jnp.float32)
        weight = weight + jnp.dot(coef, same, preferred_element_type=jnp.float32)
    lane = iota((8, 4 * TOK), 1)
    place = place + jnp.where((lane // TOK) % 2 == 1, CAP - 1.0, -1.0)
    r, lane = iota((16, 4 * TOK), 0), iota((16, 4 * TOK), 1)
    left = lane < 2 * TOK
    main_ok = left == (r < 8)
    main_slot = (r % 8).astype(jnp.float32)
    rem_ok = left == (r % 4 < 2)
    rem_slot = (8 + r % 2).astype(jnp.float32)
    main, rem = [], []
    for e in range(4):
        where = jnp.broadcast_to(place[e : e + 1], (16, 4 * TOK))
        much = jnp.broadcast_to(weight[e : e + 1], (16, 4 * TOK))
        value = jnp.where(much > 0, jnp.where(left, 1.0, much), 0.0)
        main.append(jnp.where(main_ok & (where == main_slot), value, 0.0))
        rem.append(jnp.where(rem_ok & (where == rem_slot), value, 0.0))
    return jnp.concatenate(main, axis=0), jnp.concatenate(rem, axis=0)


def pack(main, rem, data, packed):
    part = (iota((64, 4 * TOK), 0) % 16) // 4
    total = jnp.zeros((64, LANES), jnp.float32)
    for p in range(PARTS):
        lhs = jnp.concatenate([main, jnp.where(part == p, rem, 0.0)], axis=0).astype(jnp.bfloat16)
        rows = jnp.dot(
            lhs, data[:, p * LANES : (p + 1) * LANES], preferred_element_type=jnp.float32
        )
        packed[:, 16 * p : 16 * p + 16, :] = rows[:64].astype(jnp.bfloat16).reshape(4, 16, LANES)
        total = total + rows[64:]
    packed[:, 64:80, :] = total.astype(jnp.bfloat16).reshape(4, 16, LANES)


def kernel(
    fx, fg, rx, rg, routes_0, routes_1, scores_0, scores_1, gain_0, wg, wu, out_ref,
    buf, routes, scores, gain, gain_out, gain_in, raw, data, packed, weights, spare, grad,
    load_sem, local_sem, gain_sem, swap_send, swap_recv, first_sem, right_sem, left_sem, x_sem, core_sem, recv_sem,
):
    pipe = lax.axis_index("pipe")
    me = lax.axis_index("expert")
    z, x_lo, core = me // 4, (me // 2) % 2, me % 2
    q, i = z // 4, z % 4
    col = x_lo * 2 + core
    xcol = (1 - x_lo) * 2 + core
    half = i // 2

    def at(zz, xx, cc, pp=None):
        return (pipe if pp is None else pp, zz * 4 + xx * 2 + cc)

    far_pipe = pipe * (1 - core) + (lax.axis_size("pipe") - 1 - pipe) * core
    far_x = x_lo * (1 - core) + (1 - x_lo) * core
    mirror = at(z, 1 - x_lo, core, lax.axis_size("pipe") - 1 - pipe)
    core_mate = at(z, x_lo, 1 - core)
    x_mate = at(z, 1 - x_lo, core)
    z_right = at((z + 1) % 16, x_lo, core)
    z_left = at((z + 15) % 16, x_lo, core)

    barrier = pltpu.get_barrier_semaphore()

    def greet(device):
        pl.semaphore_signal(barrier, inc=1, device_id=device, device_id_type=MESH)

    greet(core_mate)
    greet(x_mate)
    greet(mirror)

    @pl.when(i > 0)
    def _():
        greet(z_left)

    @pl.when(i < 3)
    def _():
        greet(z_right)

    @pl.when(i == 0)
    def _():
        for k in range(4):
            greet(at(((q + 3) % 4) * 4 + k, far_x, core, far_pipe))
        for k in (2, 3):
            greet(at(((q + 2) % 4) * 4 + k, far_x, core, far_pipe))

    @pl.when(i == 3)
    def _():
        for k in range(4):
            greet(at(((q + 1) % 4) * 4 + k, far_x, core, far_pipe))
        for k in (0, 1):
            greet(at(((q + 2) % 4) * 4 + k, far_x, core, far_pipe))

    def load(k, source, target):
        return pltpu.make_async_copy(source, target, load_sem.at[k])

    tokens = pl.ds(pl.multiple_of(core * TOK, TOK), TOK)
    mine_to = (routes.at[core], scores.at[core], raw.at[tokens], data.at[1, tokens])
    micro = ((routes_0, scores_0, fx.at[0], fg.at[0]), (routes_1, scores_1, rx.at[0], rg.at[0]))
    load_gain = load(4, gain_0, gain)
    load_gate = load(5, wg.at[0], weights.at[:, pl.ds(0, HID)])
    load_up = load(6, wu.at[0], weights.at[:, pl.ds(HID, HID)])
    for h in range(2):

        @pl.when(core == h)
        def _():
            for k in range(4):
                load(k, micro[h][k], mine_to[k]).start()

    load_gain.start()

    pl.semaphore_wait(barrier, 7 + (i * (3 - i)) // 2)

    def remote(src, dst, send, recv, device):
        return pltpu.make_async_remote_copy(
            src_ref=src, dst_ref=dst, send_sem=send, recv_sem=recv, device_id=device, device_id_type=MESH
        )

    def swap(k, h):
        return remote(micro[1 - h][k], mine_to[k], swap_send.at[k], swap_recv.at[k], core_mate)

    for h in range(2):

        @pl.when(core == h)
        def _():
            for k in range(4):
                swap(k, h).start()

    load_gain.wait()
    gain_out[...] = gain[...]
    gain_copy = remote(gain_out, gain_in, gain_sem.at[0], gain_sem.at[1], mirror)
    gain_copy.start()
    load_gate.start()
    load_up.start()

    def piece(slot, c, h):
        return buf.at[slot, c, pl.ds(*PIECES[h])]

    def forward(slot, c, h, send, device):
        here = piece(slot, c, h)
        return remote(here, here, send, recv_sem.at[slot, c, h], device)

    def arrived(slot, c, h):
        forward(slot, c, h, core_sem.at[slot, 0], core_mate).wait_recv()

    def go_right(slot, h):
        return forward(slot, col, h, right_sem.at[slot, h], z_right)

    def go_left(slot, h):
        return forward(slot, col, h, left_sem.at[slot, h], z_left)

    def go_x(slot, h):
        return forward(slot, col, h, x_sem.at[slot, h], x_mate)

    def go_core(slot, c, which):
        whole = buf.at[slot, c]
        return remote(whole, whole, core_sem.at[slot, which], recv_sem.at[slot, c, 0], core_mate)

    def from_core(slot, c):
        go_core(slot, c, 0).wait_recv()

    far_col = far_x * 2 + core

    def first(step, zz, slot):
        return [
            remote(
                packed.at[(q + step) % 4, pl.ds(*PIECES[h])], buf.at[slot, far_col, pl.ds(*PIECES[h])],
                first_sem.at[step, h], recv_sem.at[slot, far_col, h], at(zz, far_x, core, far_pipe),
            )
            for h in range(2)
        ]

    own = 9 - i
    to_right = first(1, ((q + 1) % 4) * 4, 13 - i)
    to_left = first(3, ((q + 3) % 4) * 4 + 3, 5 - i)
    to_across = first(
        2, ((q + 2) % 4) * 4 + 3 * (1 - half), half * (17 - i) + (1 - half) * (1 - i)
    )
    to_mirror = first(0, z, own)
    keep = pltpu.make_async_copy(packed.at[q], buf.at[own, col], local_sem)

    def spread_own(h):
        @pl.when(i < 3)
        def _():
            go_right(own, h).start()

        @pl.when(i > 0)
        def _():
            go_left(own, h).start()

        go_x(own, h).start()
        if h == 1:
            go_core(own, col, 0).start()

    def here(k):
        load(k, micro[0][k], mine_to[k]).wait()
        swap(k, 0).wait_recv()

    here(0)
    here(1)
    main, rem = select_tables(routes, scores)
    here(2)
    values = raw[...].astype(jnp.float32)
    scale = lax.rsqrt(jnp.mean(values * values, axis=-1, keepdims=True) + 1e-06)

    @pl.when(core == 1)
    def _():
        gain_copy.wait_recv()
        gain[...] = gain_in[...]

    factor = gain[...]
    data[0] = (values * scale * factor).astype(jnp.bfloat16)
    here(3)
    pack(main, rem, data.reshape(4 * TOK, D), packed)
    @pl.when(core == 0)
    def _():
        keep.start()
        keep.wait()
        spread_own(0)
        spread_own(1)

    @pl.when(core == 1)
    def _():
        for copy in to_mirror:
            copy.start()

    def issue(point):
        across = 4 + half * (3 - i) + (1 - half) * i
        for copies, k, lead in (
            (to_right, 3 - i, AHEAD), (to_left, i, AHEAD), (to_across, across, 2 * AHEAD)
        ):
            due = (k <= lead) if point == 0 else (k == lead + point)

            @pl.when(due)
            def _():
                for copy in copies:
                    copy.start()

    issue(0)
    grad[...] = jnp.zeros_like(grad)

    @pl.when(core == 1)
    def _():
        for h in range(2):
            arrived(own, col, h)
            spread_own(h)

    def from_left(slot, h):
        arrived(slot, col, h)

        @pl.when(i < 3)
        def _():
            go_right(slot, h).start()

        go_x(slot, h).start()
        if h == 1:
            go_core(slot, col, 0).start()

    def from_right(slot, h):
        arrived(slot, col, h)

        @pl.when(i > 0)
        def _():
            go_left(slot, h).start()

        go_x(slot, h).start()
        if h == 1:
            go_core(slot, col, 0).start()

    def from_x(slot):
        arrived(slot, xcol, 0)
        arrived(slot, xcol, 1)
        go_core(slot, xcol, 1).start()

    def compute(base, slots, last=False):
        block = pl.ds(base, slots)
        main, rest = slots * 64, slots * 16
        for k in range(slots):
            from_core(base + k, x_lo * 2 + 1 - core)
            from_core(base + k, (1 - x_lo) * 2 + 1 - core)
        out_row, in_row = iota((main, main), 0), iota((main, main), 1)
        source = ((out_row % rest) // 4) * 16 + (out_row // rest) * 4 + out_row % 4
        turn = jnp.where(in_row == source, 1.0, 0.0).astype(jnp.bfloat16)
        tail = buf[block, :, 64:80, :].reshape(main, LANES)
        spare[:main, :] = jnp.dot(turn, tail, preferred_element_type=jnp.float32).astype(jnp.bfloat16)

        def main_of(p):
            return buf[block, :, 16 * p : 16 * p + 16, :].reshape(main, LANES)

        def rest_of(p):
            return spare[rest * p : rest * p + rest, :]

        both = []
        for size, rows_of in ((main, main_of), (rest, rest_of)):
            total = jnp.zeros((size, 2 * HID), jnp.float32)
            for p in range(PARTS):
                lanes = slice(p * LANES, (p + 1) * LANES)
                total = total + jnp.dot(rows_of(p), weights[lanes, :], preferred_element_type=jnp.float32)
            both.append(total)
        both = jnp.concatenate(both, axis=0)
        gate, up = both[:, :HID], both[:, HID:]
        hidden = gate / (1.0 + jnp.exp(-gate)) * up
        row = iota((main + rest, HID), 0)
        moved = jnp.concatenate(
            [pltpu.roll(hidden[:main], 8, 0), pltpu.roll(hidden[main:], 2, 0)], axis=0
        )
        valid = ((row < main) & (row % 16 >= 8)) | ((row >= main) & (row % 4 >= 2))
        side = jnp.where(valid, moved, 0.0).T.astype(jnp.bfloat16)
        for p in range(PARTS):
            lanes = slice(p * LANES, (p + 1) * LANES)
            total = grad[:, lanes] + jnp.dot(
                side[:, :main], main_of(p), preferred_element_type=jnp.float32
            )
            total = total + jnp.dot(side[:, main:], rest_of(p), preferred_element_type=jnp.float32)
            if last:
                out_ref[0, :, lanes] = total.astype(jnp.bfloat16)
            else:
                grad[:, lanes] = total

    load_gate.wait()
    load_up.wait()
    def along_x(step):
        if step < 0:
            from_x(own)
            return

        @pl.when(step <= 5 + i)
        def _():
            from_x(own + 1 + step)

        @pl.when(step <= 8 - i)
        def _():
            from_x(own - 1 - step)

    for step in range(9):

        for h in range(2):

            @pl.when(step <= 5 + i)
            def _():
                from_left(own + 1 + step, h)

            @pl.when(step <= 8 - i)
            def _():
                from_right(own - 1 - step, h)

        issue(step + 1)
        along_x(step - 1)
        if step == 4:
            compute(8 - 4 * half, 4)
        if step == 6:
            compute(4 + 4 * half, 4)
        if step == 7:
            compute(12 - 12 * half, 4)
        if step == 8:
            compute(2 + 10 * half, 2)
    along_x(8)
    compute(14 * half, 2, last=True)

    @pl.when(core == 0)
    def _():
        gain_copy.wait_recv()

    gain_copy.wait_send()
    for k in range(4):
        swap(k, 0).wait_send()
    for copy in to_right + to_left + to_across:
        copy.wait_send()

    @pl.when(core == 1)
    def _():
        for copy in to_mirror:
            copy.wait_send()

    for slot in range(16):
        go_core(slot, col, 0).wait_send()
        go_core(slot, xcol, 1).wait_send()
        for h in range(2):
            go_x(slot, h).wait_send()

        @pl.when((slot >= own) & (i < 3))
        def _():
            for h in range(2):
                go_right(slot, h).wait_send()

        @pl.when((slot <= own) & (i > 0))
        def _():
            for h in range(2):
                go_left(slot, h).wait_send()


def body(fx, fg, rx, rg, f_routes, r_routes, f_scores, r_scores, gain, w_gate, w_up):
    vmem, hbm = pl.BlockSpec(memory_space=pltpu.VMEM), pl.BlockSpec(memory_space=pl.ANY)
    dma = pltpu.SemaphoreType.DMA
    return pl.pallas_call(
        kernel,
        name="routed_grad",
        out_shape=pltpu.VMEM((1, HID, D), jnp.bfloat16),
        in_specs=[hbm] * 11,
        out_specs=vmem,
        scratch_shapes=[
            pltpu.VMEM((16, 4, ROWS, LANES), jnp.bfloat16),
            pltpu.VMEM((2, 8, TOK), jnp.int32),
            pltpu.VMEM((2, 8, TOK), jnp.float32),
            pltpu.VMEM((1, D), jnp.float32),
            pltpu.VMEM((1, D), jnp.float32),
            pltpu.VMEM((1, D), jnp.float32),
            pltpu.VMEM((2 * TOK, D), jnp.bfloat16),
            pltpu.VMEM((2, 2 * TOK, D), jnp.bfloat16),
            pltpu.VMEM((4, ROWS, LANES), jnp.bfloat16),
            pltpu.VMEM((D, 2 * HID), jnp.bfloat16),
            pltpu.VMEM((256, LANES), jnp.bfloat16),
            pltpu.VMEM((HID, D), jnp.float32),
            dma((7,)), dma, dma((2,)), dma((4,)), dma((4,)), dma((4, 2)), dma((16, 2)), dma((16, 2)), dma((16, 2)),
            dma((16, 2)), dma((16, 4, 2)),
        ],
        compiler_params=pltpu.CompilerParams(
            collective_id=0, has_side_effects=True, vmem_limit_bytes=63 << 20
        ),
        cost_estimate=pl.CostEstimate(flops=6 << 30, bytes_accessed=5 << 20, transcendentals=1 << 17),
    )(
        fx, fg, rx, rg, f_routes[0].T, r_routes[0].T, f_scores[0].T, r_scores[0].T, gain, w_gate, w_up
    )


def solution(mesh):
    rows = P("pipe", "expert", None)
    in_specs = (rows,) * 8 + (P("pipe", None),) + (P("pipe", None, "expert"),) * 2
    return jax.shard_map(body, mesh=mesh, in_specs=in_specs, out_specs=rows, check_vma=False)
```
